32 devices in a mesh: gx: 8 (over y, x, core), gy: 4 (over z).
Axes of the slice: x: 2, y: 2, z: 4, core: 2. Of those that a mesh axis runs over, the one named last changes fastest.
Arguments:
- u_now: float32 [3, 6, 64, 512], P(None, None, 'gx', 'gy'), may hold values from -6 to 6
- u_prev: float32 [3, 6, 64, 512], P(None, None, 'gx', 'gy'), may hold values from -6 to 6
- lame_lambda: float32 [6, 64, 512], P(None, 'gx', 'gy'), may hold values from 0.5 to 1.5
- lame_mu: float32 [6, 64, 512], P(None, 'gx', 'gy'), may hold values from 0.3 to 1
- buoyancy: float32 [6, 64, 512], P(None, 'gx', 'gy'), may hold values from 0.5 to 1
- q_now: float32 [2048, 128], P(('gx', 'gy')), may hold values from -3 to 3
- q_prev: float32 [2048, 128], P(('gx', 'gy')), may hold values from -3 to 3
- archetype: int32 [2048], P(('gx', 'gy')), may hold values from 0 to 7
- stiffness: float32 [8, 128, 128], replicated, may hold values from -1.2 to 14, as said below
- couple: float32 [8, 3, 128], replicated, may hold values from -1.5 to 1.5
- counts: int32 [8, 4, 4], P('gx'), may hold values from 1 to 16, as said below
- footprint: int32 [8, 4, 256], P('gx', 'gy'), may hold values from 0 to 1023, as said below
Outputs:
- u_last: float32 [3, 6, 64, 512], P(None, None, 'gx', 'gy')
- u_before: float32 [3, 6, 64, 512], P(None, None, 'gx', 'gy')
- q_last: float32 [2048, 128], P(('gx', 'gy'))
- q_before: float32 [2048, 128], P(('gx', 'gy'))
The draws below stay inside these ranges and needn't reach their ends.
Inputs may be any that keep to these rules, and one draw needn't show every extreme that they name: `stiffness`: symmetric, one matrix for each archetype. `counts`: at most 16; in every tile row some owner column receives 16 from every home column. `footprint`: the 4 cells of a slot form a 2 x 2 square of the home tile's surface, numbered x * 128 + y.
All inputs are finite; a program needn't handle non-finite values.
Results may differ from the reference program's by a relative error of at most 0.0001.
Values sent between devices are 32-bit elements; how exact they have to be, the bound alone decides.
A program may use at most 64 MiB of HBM per device.

```python
import functools
import math
import jax
import jax.numpy as jnp
from jax import lax

CX = 8
CY = 128
NZ = 6
SLOTS_PER_OWNER = 16
FRAME_FREEDOMS = 128
ARCH = 8
FOOTPRINT_CELLS = 4
STEPS = 2
NX = 64
NY = 512
DEVICE_SLOTS = 64
BUILDINGS = 2048
N_GX = 8
N_GY = 4


def draw_stiffness(key, part):
    key_off, key_diag = jax.random.split(jax.random.fold_in(key, 11))
    offdiag = jnp.clip(0.35 * jax.random.normal(key_off, (ARCH, FRAME_FREEDOMS, FRAME_FREEDOMS), jnp.float32), -1.2, 1.2)
    symmetric = 0.5 * (offdiag + jnp.swapaxes(offdiag, 1, 2))
    diagonal = jax.random.uniform(key_diag, (ARCH, FRAME_FREEDOMS), jnp.float32, 10.0, 14.0)
    identity = jnp.eye(FRAME_FREEDOMS, dtype=jnp.float32)
    return symmetric * (1.0 - identity) + diagonal[:, :, None] * identity


def draw_counts(key, part):
    key_base, key_full = jax.random.split(jax.random.fold_in(key, 23))
    base_counts = jax.random.randint(key_base, (N_GX, N_GY, N_GY), 1, SLOTS_PER_OWNER + 1)
    full_owner = jax.random.randint(key_full, (N_GX,), 0, N_GY)
    chosen = jnp.arange(N_GY, dtype=jnp.int32)[None, None, :] == full_owner[:, None, None]
    return jnp.where(chosen, SLOTS_PER_OWNER, base_counts).astype(jnp.int32)


def draw_footprint(key, part):
    key_x, key_y = jax.random.split(jax.random.fold_in(key, 37))
    corner_x = jax.random.randint(key_x, (N_GX, N_GY, N_GY * SLOTS_PER_OWNER, 1), 0, CX - 1)
    corner_y = jax.random.randint(key_y, (N_GX, N_GY, N_GY * SLOTS_PER_OWNER, 1), 0, CY - 1)
    corner_x = corner_x.at[:, :, 0].set(0).at[:, :, -1].set(CX - 2)
    corner_y = corner_y.at[:, :, 0].set(0).at[:, :, -1].set(CY - 2)
    offset_x = jnp.array([0, 0, 1, 1], dtype=jnp.int32)
    offset_y = jnp.array([0, 1, 0, 1], dtype=jnp.int32)
    cells = (corner_x + offset_x) * CY + (corner_y + offset_y)
    return cells.reshape(N_GX, N_GY, N_GY * SLOTS_PER_OWNER * FOOTPRINT_CELLS).astype(jnp.int32)


def touch_ends(values, rng, least, top_value):
    longest = values.shape.index(max(values.shape))
    spots = []
    for shift in (0, 1):
        where = [jax.random.randint(jax.random.fold_in(rng, axis), (), 0, length) for axis, length in enumerate(values.shape)]
        where[longest] = (where[longest] + shift) % values.shape[longest]
        spots.append(tuple(where))
    return values.at[spots[0]].set(least).at[spots[1]].set(top_value)


def levels(stream_key, extent, cuts, low, top_value):
    loudness, own = 1.0, jax.random.fold_in(stream_key, 6)
    for position, shards_of in cuts:
        draws = jnp.exp(jax.random.uniform(jax.random.fold_in(own, position), (shards_of,), jnp.float32, low / len(cuts), top_value / len(cuts)))
        loudness = loudness * jnp.repeat(draws, extent[position] // shards_of).reshape([-1 if axis == position else 1 for axis in range(len(extent))])
    return loudness


def centred(rng, dims, deviation, bound, shards=(), kind=jnp.bfloat16):
    result = jax.random.normal(rng, dims, jnp.float32) * deviation
    if len(shards) > 0:
        result = levels(rng, dims, shards, -0.22, 0.18) * result
    return jnp.clip(result, min=-bound, max=bound).astype(kind)


def setup_inputs(seed: int = 0) -> dict:
    seeds = jax.random.split(jax.random.key(seed), 13)
    u_now = centred(seeds[0], (3, NZ, NX, NY), 1.0, 6.0, ((2, 8), (3, 4)), jnp.float32)
    u_prev = centred(seeds[1], (3, NZ, NX, NY), 1.0, 6.0, ((2, 8), (3, 4)), jnp.float32)
    lame_lambda = jnp.clip(jnp.exp(math.log(1.5) - 1.0986123 * jax.random.uniform(seeds[2], (NZ, NX, NY), jnp.float32) ** levels(seeds[2], (NZ, NX, NY), ((1, 8), (2, 4)), -0.2, 0.2)), 0.5, 1.5)
    lame_mu = jnp.clip(jnp.exp(math.log(1.0) - 1.2039728 * jax.random.uniform(seeds[3], (NZ, NX, NY), jnp.float32) ** levels(seeds[3], (NZ, NX, NY), ((1, 8), (2, 4)), -0.2, 0.2)), 0.3, 1.0)
    buoyancy = jnp.clip(jnp.exp(math.log(1.0) - 0.6931472 * jax.random.uniform(seeds[4], (NZ, NX, NY), jnp.float32) ** levels(seeds[4], (NZ, NX, NY), ((1, 8), (2, 4)), -0.2, 0.2)), 0.5, 1.0)
    q_now = centred(seeds[5], (BUILDINGS, FRAME_FREEDOMS), 0.5, 3.0, ((0, 32),), jnp.float32)
    q_prev = centred(seeds[6], (BUILDINGS, FRAME_FREEDOMS), 0.5, 3.0, ((0, 32),), jnp.float32)
    archetype = touch_ends(jax.random.randint(seeds[7], (BUILDINGS,), 0, ARCH), jax.random.fold_in(seeds[7], 1), 0, ARCH - 1).astype(jnp.int32)
    stiffness = draw_stiffness(jax.random.fold_in(seeds[12], 71), 0)
    couple = centred(seeds[9], (ARCH, 3, FRAME_FREEDOMS), 0.3, 1.5, (), jnp.float32)
    counts = draw_counts(jax.random.fold_in(seeds[12], 71), 0)
    footprint = draw_footprint(jax.random.fold_in(seeds[12], 71), 0)
    return {"u_now": u_now, "u_prev": u_prev, "lame_lambda": lame_lambda, "lame_mu": lame_mu, "buoyancy": buoyancy, "q_now": q_now, "q_prev": q_prev, "archetype": archetype, "stiffness": stiffness, "couple": couple, "counts": counts, "footprint": footprint}


time_step = 0.25


def derive(padded, along):
    field = padded
    for other in (1, 2, 3):
        if other != along:
            field = lax.slice_in_dim(field, 2, field.shape[other] - 2, axis=other)
    length = field.shape[along] - 4

    def window(offset):
        return lax.slice_in_dim(field, offset, offset + length, axis=along)

    return (8.0 * (window(3) - window(1)) - (window(4) - window(0))) / 12.0


def stress_of(padded, lam_field, mu_field):
    grad_x = derive(padded, 2)
    grad_y = derive(padded, 3)
    grad_z = derive(padded, 1)
    trace = grad_x[0] + grad_y[1] + grad_z[2]
    return jnp.stack([
        lam_field * trace + 2.0 * mu_field * grad_x[0],
        lam_field * trace + 2.0 * mu_field * grad_y[1],
        lam_field * trace + 2.0 * mu_field * grad_z[2],
        mu_field * (grad_y[0] + grad_x[1]),
        mu_field * (grad_z[0] + grad_x[2]),
        mu_field * (grad_z[1] + grad_y[2])])


def divergence(padded):
    grad_x = derive(padded, 2)
    grad_y = derive(padded, 3)
    grad_z = derive(padded, 1)
    return jnp.stack([
        grad_x[0] + grad_y[3] + grad_z[4],
        grad_x[3] + grad_y[1] + grad_z[5],
        grad_x[4] + grad_y[5] + grad_z[2]])


def building_group(stiffness, couple, inputs):
    frame_state, prior_frame_state, kinds, ground_motion = inputs
    stiff_sel = stiffness[kinds]
    couple_sel = couple[kinds]
    highest = lax.Precision.HIGHEST
    stiff_term = jnp.einsum('bij,bj->bi', stiff_sel, frame_state, precision=highest)
    shear_force = jnp.einsum('bcj,bj->bc', couple_sel, frame_state, precision=highest)
    drive = jnp.einsum('bcj,bc->bj', couple_sel, ground_motion, precision=highest)
    next_frame_state = 2.0 * frame_state - prior_frame_state + (time_step * time_step) * (drive - stiff_term)
    return next_frame_state, shear_force


def scatter_tile(cells, contrib):
    return jnp.zeros((3, CX * CY), jnp.float32).at[:, cells].add(contrib)


def reference(u_now, u_prev, lame_lambda, lame_mu, buoyancy, q_now, q_prev, archetype, stiffness, couple, counts, footprint):
    building_groups = N_GX * N_GY
    building_slot_index = jnp.arange(SLOTS_PER_OWNER, dtype=jnp.int32)
    active_slots = (building_slot_index[None, None, None, :] < counts[:, :, :, None]).astype(jnp.float32).reshape(N_GX, N_GY, DEVICE_SLOTS)
    index_padded_wide = jnp.broadcast_to(footprint[:, :, None, :], (N_GX, N_GY, 3, DEVICE_SLOTS * FOOTPRINT_CELLS))
    field, older = u_now, u_prev
    frame_state, prior_frame_state = q_now, q_prev
    advance_group = functools.partial(building_group, stiffness, couple)
    scatter_all = jax.vmap(jax.vmap(scatter_tile))
    for counter in range(STEPS):
        surface = field[:, 0].reshape(3, N_GX, CX, N_GY, CY).transpose(1, 3, 0, 2, 4).reshape(N_GX, N_GY, 3, CX * CY)
        entry_values = jnp.take_along_axis(surface, index_padded_wide, axis=3)
        base_layer = entry_values.reshape(N_GX, N_GY, 3, DEVICE_SLOTS, FOOTPRINT_CELLS).sum(axis=4) / FOOTPRINT_CELLS * active_slots[:, :, None, :]
        ground_motion = base_layer.reshape(N_GX, N_GY, 3, N_GY, SLOTS_PER_OWNER).transpose(0, 3, 1, 4, 2).reshape(building_groups, DEVICE_SLOTS, 3)
        next_frame_state, shear_force = lax.map(advance_group, (frame_state.reshape(building_groups, DEVICE_SLOTS, FRAME_FREEDOMS), prior_frame_state.reshape(building_groups, DEVICE_SLOTS, FRAME_FREEDOMS), archetype.reshape(building_groups, DEVICE_SLOTS), ground_motion))
        home_shear_force = shear_force.reshape(N_GX, N_GY, N_GY, SLOTS_PER_OWNER, 3).transpose(0, 2, 4, 1, 3).reshape(N_GX, N_GY, 3, DEVICE_SLOTS) * active_slots[:, :, None, :]
        contrib = jnp.repeat(home_shear_force / FOOTPRINT_CELLS, FOOTPRINT_CELLS, axis=3)
        force_tiles = scatter_all(footprint, contrib)
        force = force_tiles.reshape(N_GX, N_GY, 3, CX, CY).transpose(2, 0, 3, 1, 4).reshape(3, NX, NY)
        padded = jnp.pad(field, ((0, 0), (2, 2), (2, 2), (2, 2)))
        stress = stress_of(padded, lame_lambda, lame_mu)
        total = divergence(jnp.pad(stress, ((0, 0), (2, 2), (2, 2), (2, 2))))
        total = total.at[:, 0].add(force)
        field_new = 2.0 * field - older + (time_step * time_step) * (buoyancy * total)
        older, field = field, field_new
        prior_frame_state, frame_state = frame_state, next_frame_state.reshape(BUILDINGS, FRAME_FREEDOMS)
    return field, older, frame_state, prior_frame_state
```

```python
import functools

import jax
import jax.numpy as jnp
from jax import lax
from jax.experimental import pallas as pl
from jax.experimental.pallas import tpu as pltpu
from jax.sharding import PartitionSpec as P

FOOTPRINT_CELLS = 4
STEPS = 2
TIME_STEP = 0.25
RIM = 4
MESH = pl.DeviceIdType.MESH
F32 = jnp.float32
BF16 = jnp.bfloat16

X_DIRS = ((1, 0), (-1, 0))
Y_DIRS = ((-1, 1), (-1, -1), (0, 1), (0, -1), (1, 1), (1, -1))


def iota(shape, dim):
    return lax.broadcasted_iota(jnp.int32, shape, dim)


def split(value):
    high = value.astype(BF16)
    return high, (value - high.astype(F32)).astype(BF16)


def pack_x(fields):
    half = fields.shape[0] // 2
    first, second = fields[:half], fields[half:]
    upper = iota((1, 8, 128), 1) < RIM
    to_next = jnp.where(upper, pltpu.roll(first, RIM, 1), second)
    to_before = jnp.where(upper, first, pltpu.roll(second, RIM, 1))
    return to_next, to_before


def unpack_x(from_before, from_next):
    upper = iota((1, 8, 128), 1) < RIM
    first = jnp.where(upper, from_next, pltpu.roll(from_before, RIM, 1))
    second = jnp.where(upper, pltpu.roll(from_next, RIM, 1), from_before)
    return jnp.concatenate([first, second], axis=0)


def pack_y(fields):
    count = fields.shape[0]
    lane = iota((8, 128), 1)
    tiles = []
    for start in range(0, count, 16):
        tile = jnp.zeros((8, 128), F32)
        for k in range(start, min(start + 16, count)):
            place = 8 * (k - start)
            moved = pltpu.roll(fields[k], (place + RIM) % 128, 1)
            tile = jnp.where((lane >= place) & (lane < place + 8), moved, tile)
        tiles.append(tile)
    return jnp.stack(tiles)


def unpack_y(tiles, count):
    slabs = []
    for k in range(count):
        slabs.append(pltpu.roll(tiles[k // 16], (124 - 8 * (k % 16)) % 128, 1))
    return jnp.stack(slabs)


def slope(here, other, axis, both):
    size = here.shape[axis]
    place = iota((1,) * (axis - 0) + (size,) + (1,) * (here.ndim - axis - 1), axis)
    shape = [1] * (here.ndim - 2) + [8, 128]
    place = iota(tuple(shape), axis)
    results = []
    moved = {}
    for shift in (1, -1, 2, -2):
        amount = (-shift) % size
        moved[shift] = (pltpu.roll(here, amount, axis), pltpu.roll(other, amount, axis))

    def pick(shift, swap):
        mine, theirs = moved[shift]
        if swap:
            mine, theirs = theirs, mine
        wrapped = place >= size - shift if shift > 0 else place < -shift
        return jnp.where(wrapped, theirs, mine)

    for swap in (False, True) if both else (False,):
        results.append(
            8.0 * (pick(1, swap) - pick(-1, swap)) - (pick(2, swap) - pick(-2, swap))
        )
    return results if both else results[0]


def slope_z(field):
    nothing = jnp.zeros((2,) + field.shape[1:], F32)
    padded = jnp.concatenate([nothing, field, nothing], axis=0)
    n = field.shape[0]
    return 8.0 * (padded[3 : n + 3] - padded[1 : n + 1]) - (padded[4 : n + 4] - padded[:n])


def divergence(u, rim_x, rim_y, corner, lam, mu, lam_x, mu_x, lam_y, mu_y):
    ux, uy, uz = u[0], u[1], u[2]
    x_x, x_xh = slope(ux, rim_x[0], 1, True)
    y_x, y_xh = slope(uy, rim_x[1], 1, True)
    z_x, z_xh = slope(uz, rim_x[2], 1, True)
    x_y, x_yh = slope(ux, rim_y[0], 2, True)
    y_y, y_yh = slope(uy, rim_y[1], 2, True)
    z_y, z_yh = slope(uz, rim_y[2], 2, True)
    x_z, y_z, z_z = slope_z(ux), slope_z(uy), slope_z(uz)
    spread = lam * (x_x + y_y + z_z)
    s_xx = spread + 2.0 * mu * x_x
    s_yy = spread + 2.0 * mu * y_y
    s_zz = spread + 2.0 * mu * z_z
    s_xy = mu * (x_y + y_x)
    s_xz = mu * (x_z + z_x)
    s_yz = mu * (y_z + z_y)
    x_yr = slope(rim_x[0], corner[0], 2, False)
    y_yr = slope(rim_x[1], corner[1], 2, False)
    x_zr, z_zr = slope_z(rim_x[0]), slope_z(rim_x[2])
    s_xx_r = lam_x * (x_xh + y_yr + z_zr) + 2.0 * mu_x * x_xh
    s_xy_r = mu_x * (x_yr + y_xh)
    s_xz_r = mu_x * (x_zr + z_xh)
    x_xc = slope(rim_y[0], corner[0], 1, False)
    y_xc = slope(rim_y[1], corner[1], 1, False)
    y_zc, z_zc = slope_z(rim_y[1]), slope_z(rim_y[2])
    s_yy_c = lam_y * (x_xc + y_yh + z_zc) + 2.0 * mu_y * y_yh
    s_xy_c = mu_y * (x_yh + y_xc)
    s_yz_c = mu_y * (y_zc + z_yh)
    total_x = slope(s_xx, s_xx_r, 1, False) + slope(s_xy, s_xy_c, 2, False) + slope_z(s_xz)
    total_y = slope(s_xy, s_xy_r, 1, False) + slope(s_yy, s_yy_c, 2, False) + slope_z(s_yz)
    total_z = slope(s_xz, s_xz_r, 1, False) + slope(s_yz, s_yz_c, 2, False) + slope_z(s_zz)
    return jnp.stack([total_x, total_y, total_z])


def kernel(
    rows,
    owners,
    u_ref,
    u_prev_ref,
    lam_ref,
    mu_ref,
    buoy_ref,
    q_ref,
    q_prev_ref,
    arch_ref,
    stiff_ref,
    couple_ref,
    counts_ref,
    cells_ref,
    u_last_ref,
    u_before_ref,
    q_last_ref,
    q_before_ref,
    xs0,
    xs1,
    xr0,
    xr1,
    ys,
    yr,
    bs,
    br,
    table,
    x_send,
    x_recv,
    y_send,
    y_recv,
    b_send,
    b_recv,
):
    r, h = lax.axis_index("gx"), lax.axis_index("gy")
    nz = lam_ref.shape[0]
    slots = q_ref.shape[0]
    capacity = slots // owners
    kinds = stiff_ref.shape[0]
    freedoms = q_ref.shape[1]
    xs, xr = (xs0, xs1), (xr0, xr1)

    def target(direction):
        dx, dy = direction
        there = None
        for d, me, n in ((dx, r, rows), (dy, h, owners)):
            if d:
                ok = me + d < n if d > 0 else me > 0
                there = ok if there is None else there & ok
        return there, (r + dx, h + dy)

    def source(direction):
        return target((-direction[0], -direction[1]))

    peers = X_DIRS + tuple(d for d in Y_DIRS if d[0])

    for slot, direction in enumerate(X_DIRS):
        there, _ = source(direction)

        @pl.when(jnp.logical_not(there))
        def _(slot=slot):
            for buffer in xr:
                buffer[slot] = jnp.zeros(buffer.shape[1:], F32)

    for slot, direction in enumerate(Y_DIRS):
        there, _ = source(direction)

        @pl.when(jnp.logical_not(there))
        def _(slot=slot):
            for turn in range(STEPS):
                yr[turn, slot] = jnp.zeros(yr.shape[2:], F32)

    barrier = pltpu.get_barrier_semaphore()
    arrivals = jnp.int32(owners - 1)
    for direction in peers:
        there, device = target(direction)
        arrivals = arrivals + there.astype(jnp.int32)

        @pl.when(there)
        def _(device=device):
            pl.semaphore_signal(barrier, inc=1, device_id=device, device_id_type=MESH)

    for step in range(1, owners):
        other = lax.rem(h + step, owners)
        pl.semaphore_signal(barrier, inc=1, device_id=(r, other), device_id_type=MESH)

    def x_copy(turn, slot, device):
        return pltpu.make_async_remote_copy(
            src_ref=xs[turn].at[slot],
            dst_ref=xr[turn].at[slot],
            send_sem=x_send.at[turn, slot],
            recv_sem=x_recv.at[turn, slot],
            device_id=device,
            device_id_type=MESH,
        )

    def y_copy(turn, slot, device):
        return pltpu.make_async_remote_copy(
            src_ref=ys.at[turn],
            dst_ref=yr.at[turn, slot],
            send_sem=y_send.at[turn, slot],
            recv_sem=y_recv.at[turn, slot],
            device_id=device,
            device_id_type=MESH,
        )

    def b_copy(turn, step):
        other = lax.rem(h + step, owners)
        return pltpu.make_async_remote_copy(
            src_ref=bs.at[turn, other],
            dst_ref=br.at[turn, h],
            send_sem=b_send.at[turn, step],
            recv_sem=b_recv.at[turn, step],
            device_id=(r, other),
            device_id_type=MESH,
        )

    def b_arrival(turn, step):
        other = lax.rem(h + owners - step, owners)
        return pltpu.make_async_remote_copy(
            src_ref=bs.at[turn, other],
            dst_ref=br.at[turn, other],
            send_sem=b_send.at[turn, step],
            recv_sem=b_recv.at[turn, step],
            device_id=(r, other),
            device_id_type=MESH,
        )

    def send_rims(turn):
        for copy, dirs in ((x_copy, X_DIRS), (y_copy, Y_DIRS)):
            for slot, direction in enumerate(dirs):
                there, device = target(direction)

                @pl.when(there)
                def _(copy=copy, slot=slot, device=device):
                    copy(turn, slot, device).start()

    def wait_rims(turn):
        for copy, dirs in ((x_copy, X_DIRS), (y_copy, Y_DIRS)):
            for slot, direction in enumerate(dirs):
                there, device = source(direction)

                @pl.when(there)
                def _(copy=copy, slot=slot, device=device):
                    copy(turn, slot, device).wait_recv()

    def wait_sends(turn):
        for copy, dirs in ((x_copy, X_DIRS), (y_copy, Y_DIRS)):
            for slot, direction in enumerate(dirs):
                there, device = target(direction)

                @pl.when(there)
                def _(copy=copy, slot=slot, device=device):
                    copy(turn, slot, device).wait_send()

        for step in range(1, owners):
            b_copy(turn, step).wait_send()

    def put_rims(turn, fields):
        to_next, to_before = pack_x(fields)
        xs[turn][0] = to_next
        xs[turn][1] = to_before
        tiles = pack_y(fields)
        ys[turn, : tiles.shape[0]] = tiles

    def take_rims(turn, count):
        rim_x = unpack_x(xr[turn][0], xr[turn][1])
        column = (iota((1, 8, 128), 2) & 7) < RIM
        before = jnp.where(column, yr[turn, 4], yr[turn, 5])
        beside = jnp.where(column, yr[turn, 2], yr[turn, 3])
        after = jnp.where(column, yr[turn, 0], yr[turn, 1])
        corner = jnp.where(iota((1, 8, 128), 1) < RIM, after, before)
        return rim_x, unpack_y(beside, count), unpack_y(corner, 3 * nz)

    u = u_ref[...]
    lam, mu = lam_ref[...] * (1.0 / 144.0), mu_ref[...] * (1.0 / 144.0)
    put_rims(0, jnp.concatenate([u.reshape(3 * nz, 8, 128), lam, mu], axis=0))
    pl.semaphore_wait(barrier, arrivals)
    send_rims(0)

    cells = cells_ref[0].astype(F32)
    wide = (slots, slots * FOOTPRINT_CELLS)
    own = (iota(wide, 1) // FOOTPRINT_CELLS) == iota(wide, 0)
    corner_cell = jnp.min(jnp.where(own, cells, 1e9), axis=1, keepdims=True)
    corner_x = jnp.floor(corner_cell * (1.0 / 128.0))
    corner_y = corner_cell - 128.0 * corner_x
    lane = iota((slots, 128), 1)
    along_y = lane.astype(F32) - corner_y
    window_y = ((along_y == 0.0) | (along_y == 1.0)).astype(F32).astype(BF16)
    along_x = (lane & 7).astype(F32) - corner_x
    part = lane & 31
    slot_row = iota((slots, 1), 0)
    live_count = jnp.zeros((slots, 1), jnp.int32)
    for o in range(owners):
        live_count = jnp.where(slot_row // capacity == o, counts_ref[0, h, o], live_count)
    live = (slot_row % capacity) < live_count
    weight = jnp.where(
        live & ((along_x == 0.0) | (along_x == 1.0)) & (part < 24), 1.0 / FOOTPRINT_CELLS, 0.0
    )
    square = (slots, slots)
    arch = jnp.sum(
        jnp.where(iota(square, 0) == iota(square, 1), arch_ref[...].astype(F32), 0.0),
        axis=1,
        keepdims=True,
    )
    is_kind = [arch == float(a) for a in range(kinds)]
    coupling = []
    for c in range(3):
        chosen = jnp.zeros((slots, freedoms), F32)
        for a in range(kinds):
            chosen = jnp.where(is_kind[a], couple_ref[a, c : c + 1, :], chosen)
        coupling.append(chosen)

    def surface_motion(field):
        surface = field[:, 0]
        high = surface.astype(BF16).astype(F32)
        nothing = jnp.zeros((8, 128), F32)
        stacked = jnp.concatenate(
            [high.reshape(24, 128), nothing, (surface - high).reshape(24, 128), nothing]
            + [nothing] * 8,
            axis=0,
        ).astype(BF16)
        gathered = lax.dot_general(
            window_y, stacked, (((1,), (1,)), ((), ())), preferred_element_type=F32
        )
        return gathered * weight

    def base_shear(state):
        shear = [jnp.sum(coupling[c] * state, axis=1, keepdims=True) for c in range(3)]
        return jnp.where(part < 8, shear[0], jnp.where(part < 16, shear[1], shear[2]))

    def send_buildings(turn, field, state):
        both = jnp.where(lane < 64, surface_motion(field), base_shear(state))
        both = both.reshape(owners, capacity, 128)
        bs[turn] = both
        br[turn, h] = bs[turn, h]
        for step in range(1, owners):
            b_copy(turn, step).start()

    def take_buildings(turn):
        for step in range(1, owners):
            b_arrival(turn, step).wait_recv()
        both = br[turn].reshape(slots, 128)
        drive = jnp.zeros((slots, freedoms), F32)
        for c in range(3):
            mine = (lane < 64) & (part >= 8 * c) & (part < 8 * c + 8)
            base = jnp.sum(jnp.where(mine, both, 0.0), axis=1, keepdims=True)
            drive = drive + coupling[c] * base
        pull = both * weight
        high = pull.astype(BF16).astype(F32)
        pull = jnp.where((lane & 32) == 0, high, pull - high)
        spread = lax.dot_general(
            pull.T.astype(BF16), window_y, (((1,), (0,)), ((), ())), preferred_element_type=F32
        )
        force = (spread[64:88] + spread[96:120]).reshape(3, 8, 128)
        return drive, force

    def stiff_term(state):
        high, low = split(state)
        stacked = jnp.concatenate([high.astype(F32), low.astype(F32)], axis=0)
        twice = jnp.concatenate([arch, arch], axis=0)
        spread = jnp.concatenate(
            [jnp.where(twice == float(a), stacked, 0.0).astype(BF16) for a in range(kinds)],
            axis=1,
        )
        product = jnp.dot(spread, table[...], preferred_element_type=F32)
        product = product[:, :freedoms] + product[:, freedoms:]
        return product[:slots] + product[slots:]

    q = q_ref[...]
    send_buildings(0, u, q)
    stiff_high, stiff_low = split(stiff_ref[...].reshape(kinds * freedoms, freedoms))
    table[:, :freedoms] = stiff_high
    table[:, freedoms:] = stiff_low
    stiff = stiff_term(q)
    u_old, q_old = u_prev_ref[...], q_prev_ref[...]
    gain = buoy_ref[...] * (TIME_STEP * TIME_STEP)
    count = 5 * nz
    lam_mu_x = lam_mu_y = None
    for turn in range(STEPS):
        drive, force = take_buildings(turn)
        q, q_old = 2.0 * q - q_old + (TIME_STEP * TIME_STEP) * (drive - stiff), q
        wait_rims(turn)
        rim_x, rim_y, corner = take_rims(turn, count)
        if turn == 0:
            lam_mu_x, lam_mu_y = rim_x[3 * nz :], rim_y[3 * nz :]
        shape = (3, nz, 8, 128)
        total = divergence(
            u,
            rim_x[: 3 * nz].reshape(shape),
            rim_y[: 3 * nz].reshape(shape),
            corner.reshape(shape),
            lam,
            mu,
            lam_mu_x[:nz],
            lam_mu_x[nz:],
            lam_mu_y[:nz],
            lam_mu_y[nz:],
        )
        total = jnp.concatenate([total[:, :1] + force[:, None], total[:, 1:]], axis=1)
        u, u_old = 2.0 * u - u_old + gain * total, u
        count = 3 * nz
        if turn + 1 < STEPS:
            put_rims(turn + 1, u.reshape(3 * nz, 8, 128))
            send_rims(turn + 1)
            send_buildings(turn + 1, u, q)
            u_before_ref[...] = u
            q_before_ref[...] = q
            stiff = stiff_term(q)
    u_last_ref[...] = u
    q_last_ref[...] = q
    for turn in range(STEPS):
        wait_sends(turn)


def shards(
    rows,
    owners,
    u_now,
    u_prev,
    lame_lambda,
    lame_mu,
    buoyancy,
    q_now,
    q_prev,
    archetype,
    stiffness,
    couple,
    counts,
    footprint,
):
    nz = lame_mu.shape[0]
    slots, freedoms = q_now.shape
    capacity = slots // owners
    kinds = stiffness.shape[0]
    pairs = (5 * nz) // 2, (3 * nz) // 2
    vmem = pl.BlockSpec(memory_space=pltpu.VMEM)
    smem = pl.BlockSpec(memory_space=pltpu.SMEM)
    dma = pltpu.SemaphoreType.DMA
    return pl.pallas_call(
        functools.partial(kernel, rows, owners),
        out_shape=(
            jax.ShapeDtypeStruct(u_now.shape, F32),
            jax.ShapeDtypeStruct(u_now.shape, F32),
            jax.ShapeDtypeStruct(q_now.shape, F32),
            jax.ShapeDtypeStruct(q_now.shape, F32),
        ),
        in_specs=[vmem] * 10 + [smem, vmem],
        out_specs=(vmem,) * 4,
        scratch_shapes=[
            pltpu.VMEM((2, pairs[0], 8, 128), F32),
            pltpu.VMEM((2, pairs[1], 8, 128), F32),
            pltpu.VMEM((2, pairs[0], 8, 128), F32),
            pltpu.VMEM((2, pairs[1], 8, 128), F32),
            pltpu.VMEM((STEPS, 2, 8, 128), F32),
            pltpu.VMEM((STEPS, len(Y_DIRS), 2, 8, 128), F32),
            pltpu.VMEM((STEPS, owners, capacity, 128), F32),
            pltpu.VMEM((STEPS, owners, capacity, 128), F32),
            pltpu.VMEM((kinds * freedoms, 2 * freedoms), BF16),
            dma((STEPS, 2)),
            dma((STEPS, 2)),
            dma((STEPS, len(Y_DIRS))),
            dma((STEPS, len(Y_DIRS))),
            dma((STEPS, owners)),
            dma((STEPS, owners)),
        ],
        compiler_params=pltpu.CompilerParams(
            collective_id=0, has_side_effects=True, vmem_limit_bytes=32 * 1024 * 1024
        ),
    )(
        u_now,
        u_prev,
        lame_lambda,
        lame_mu,
        buoyancy,
        q_now,
        q_prev,
        archetype.reshape(1, slots),
        stiffness,
        couple,
        counts,
        footprint,
    )


def solution(mesh):
    return jax.shard_map(
        functools.partial(shards, mesh.shape["gx"], mesh.shape["gy"]),
        mesh=mesh,
        in_specs=(
            P(None, None, "gx", "gy"),
            P(None, None, "gx", "gy"),
            P(None, "gx", "gy"),
            P(None, "gx", "gy"),
            P(None, "gx", "gy"),
            P(("gx", "gy"), None),
            P(("gx", "gy"), None),
            P(("gx", "gy")),
            P(),
            P(),
            P("gx", None, None),
            P("gx", "gy", None),
        ),
        out_specs=(
            P(None, None, "gx", "gy"),
            P(None, None, "gx", "gy"),
            P(("gx", "gy"), None),
            P(("gx", "gy"), None),
        ),
        check_vma=False,
    )
```

```python
import functools

import jax
import jax.numpy as jnp
from jax import lax
from jax.experimental import pallas as pl
from jax.experimental.pallas import tpu as pltpu
from jax.sharding import PartitionSpec as P

FOOTPRINT_CELLS = 4
STEPS = 2
TIME_STEP = 0.25
RIM = 4
MESH = pl.DeviceIdType.MESH
F32 = jnp.float32
BF16 = jnp.bfloat16

X_DIRS = ((1, 0), (-1, 0))
Y_DIRS = ((-1, 1), (-1, -1), (0, 1), (0, -1), (1, 1), (1, -1))


def iota(shape, dim):
    return lax.broadcasted_iota(jnp.int32, shape, dim)


def split(value):
    high = value.astype(BF16)
    return high, (value - high.astype(F32)).astype(BF16)


def pack_x(fields):
    half = fields.shape[0] // 2
    first, second = fields[:half], fields[half:]
    upper = iota((1, 8, 128), 1) < RIM
    to_next = jnp.where(upper, pltpu.roll(first, RIM, 1), second)
    to_before = jnp.where(upper, first, pltpu.roll(second, RIM, 1))
    return to_next, to_before


def unpack_x(from_before, from_next):
    upper = iota((1, 8, 128), 1) < RIM
    first = jnp.where(upper, from_next, pltpu.roll(from_before, RIM, 1))
    second = jnp.where(upper, pltpu.roll(from_next, RIM, 1), from_before)
    return jnp.concatenate([first, second], axis=0)


def pack_y(fields):
    count = fields.shape[0]
    lane = iota((8, 128), 1)
    tiles = []
    for start in range(0, count, 16):
        tile = jnp.zeros((8, 128), F32)
        for k in range(start, min(start + 16, count)):
            place = 8 * (k - start)
            moved = pltpu.roll(fields[k], (place + RIM) % 128, 1)
            tile = jnp.where((lane >= place) & (lane < place + 8), moved, tile)
        tiles.append(tile)
    return jnp.stack(tiles)


def unpack_y(tiles, count):
    slabs = []
    for k in range(count):
        slabs.append(pltpu.roll(tiles[k // 16], (124 - 8 * (k % 16)) % 128, 1))
    return jnp.stack(slabs)


def slope(here, other, axis, both):
    size = here.shape[axis]
    place = iota((1,) * (here.ndim - 2) + (8, 128), axis)

    def shifted(mine, theirs, shift):
        entering = place < shift if shift > 0 else place >= size + shift
        return pltpu.roll(jnp.where(entering, theirs, mine), (-shift) % size, axis)

    def slope_of(mine, theirs):
        return 8.0 * (shifted(mine, theirs, 1) - shifted(mine, theirs, -1)) - (
            shifted(mine, theirs, 2) - shifted(mine, theirs, -2)
        )

    if both:
        return slope_of(here, other), slope_of(other, here)
    return slope_of(here, other)


def slope_z(field):
    nothing = jnp.zeros((2,) + field.shape[1:], F32)
    padded = jnp.concatenate([nothing, field, nothing], axis=0)
    n = field.shape[0]
    return 8.0 * (padded[3 : n + 3] - padded[1 : n + 1]) - (padded[4 : n + 4] - padded[:n])


def divergence(u, rim_x, rim_y, corner, lam, mu, lam_x, mu_x, lam_y, mu_y):
    ux, uy, uz = u[0], u[1], u[2]
    x_x, x_xh = slope(ux, rim_x[0], 1, True)
    y_x, y_xh = slope(uy, rim_x[1], 1, True)
    z_x, z_xh = slope(uz, rim_x[2], 1, True)
    x_y, x_yh = slope(ux, rim_y[0], 2, True)
    y_y, y_yh = slope(uy, rim_y[1], 2, True)
    z_y, z_yh = slope(uz, rim_y[2], 2, True)
    x_z, y_z, z_z = slope_z(ux), slope_z(uy), slope_z(uz)
    spread = lam * (x_x + y_y + z_z)
    s_xx = spread + 2.0 * mu * x_x
    s_yy = spread + 2.0 * mu * y_y
    s_zz = spread + 2.0 * mu * z_z
    s_xy = mu * (x_y + y_x)
    s_xz = mu * (x_z + z_x)
    s_yz = mu * (y_z + z_y)
    x_yr = slope(rim_x[0], corner[0], 2, False)
    y_yr = slope(rim_x[1], corner[1], 2, False)
    x_zr, z_zr = slope_z(rim_x[0]), slope_z(rim_x[2])
    s_xx_r = lam_x * (x_xh + y_yr + z_zr) + 2.0 * mu_x * x_xh
    s_xy_r = mu_x * (x_yr + y_xh)
    s_xz_r = mu_x * (x_zr + z_xh)
    x_xc = slope(rim_y[0], corner[0], 1, False)
    y_xc = slope(rim_y[1], corner[1], 1, False)
    y_zc, z_zc = slope_z(rim_y[1]), slope_z(rim_y[2])
    s_yy_c = lam_y * (x_xc + y_yh + z_zc) + 2.0 * mu_y * y_yh
    s_xy_c = mu_y * (x_yh + y_xc)
    s_yz_c = mu_y * (y_zc + z_yh)
    total_x = slope(s_xx, s_xx_r, 1, False) + slope(s_xy, s_xy_c, 2, False) + slope_z(s_xz)
    total_y = slope(s_xy, s_xy_r, 1, False) + slope(s_yy, s_yy_c, 2, False) + slope_z(s_yz)
    total_z = slope(s_xz, s_xz_r, 1, False) + slope(s_yz, s_yz_c, 2, False) + slope_z(s_zz)
    return jnp.stack([total_x, total_y, total_z])


def kernel(
    rows,
    owners,
    u_hbm,
    u_prev_hbm,
    lam_hbm,
    mu_hbm,
    buoy_hbm,
    q_hbm,
    q_prev_hbm,
    arch_hbm,
    stiff_hbm,
    couple_hbm,
    counts_hbm,
    cells_hbm,
    u_last_ref,
    u_before_ref,
    q_last_ref,
    q_before_ref,
    xs0,
    xs1,
    xr0,
    xr1,
    ys,
    yr,
    bs,
    br,
    table,
    u_ref,
    u_prev_ref,
    lam_ref,
    mu_ref,
    buoy_ref,
    q_ref,
    q_prev_ref,
    arch_ref,
    stiff_ref,
    couple_ref,
    counts_ref,
    cells_ref,
    loaded,
    x_send,
    x_recv,
    y_send,
    y_recv,
    b_send,
    b_recv,
):
    r, h = lax.axis_index("gx"), lax.axis_index("gy")
    nz = lam_ref.shape[0]
    slots = q_ref.shape[0]
    capacity = slots // owners
    kinds = stiff_ref.shape[0]
    freedoms = q_ref.shape[1]
    xs, xr = (xs0, xs1), (xr0, xr1)

    def target(direction):
        dx, dy = direction
        there = None
        for d, me, n in ((dx, r, rows), (dy, h, owners)):
            if d:
                ok = me + d < n if d > 0 else me > 0
                there = ok if there is None else there & ok
        return there, (r + dx, h + dy)

    def source(direction):
        return target((-direction[0], -direction[1]))

    peers = X_DIRS + tuple(d for d in Y_DIRS if d[0])

    for slot, direction in enumerate(X_DIRS):
        there, _ = source(direction)

        @pl.when(jnp.logical_not(there))
        def _(slot=slot):
            for buffer in xr:
                buffer[slot] = jnp.zeros(buffer.shape[1:], F32)

    for slot, direction in enumerate(Y_DIRS):
        there, _ = source(direction)

        @pl.when(jnp.logical_not(there))
        def _(slot=slot):
            for turn in range(STEPS):
                yr[turn, slot] = jnp.zeros(yr.shape[2:], F32)

    barrier = pltpu.get_barrier_semaphore()
    arrivals = jnp.int32(owners - 1)
    for direction in peers:
        there, device = target(direction)
        arrivals = arrivals + there.astype(jnp.int32)

        @pl.when(there)
        def _(device=device):
            pl.semaphore_signal(barrier, inc=1, device_id=device, device_id_type=MESH)

    for step in range(1, owners):
        other = lax.rem(h + step, owners)
        pl.semaphore_signal(barrier, inc=1, device_id=(r, other), device_id_type=MESH)

    loads = {}
    for source_ref, ref in (
        (u_hbm, u_ref),
        (lam_hbm, lam_ref),
        (mu_hbm, mu_ref),
        (cells_hbm, cells_ref),
        (counts_hbm, counts_ref),
        (q_hbm, q_ref),
        (arch_hbm, arch_ref),
        (couple_hbm, couple_ref),
        (stiff_hbm, stiff_ref),
        (q_prev_hbm, q_prev_ref),
        (u_prev_hbm, u_prev_ref),
        (buoy_hbm, buoy_ref),
    ):
        copy = pltpu.make_async_copy(source_ref, ref, loaded.at[len(loads)])
        copy.start()
        loads[id(ref)] = copy

    def load(ref):
        loads[id(ref)].wait()
        return ref[...]

    def x_copy(turn, slot, device):
        return pltpu.make_async_remote_copy(
            src_ref=xs[turn].at[slot],
            dst_ref=xr[turn].at[slot],
            send_sem=x_send.at[turn, slot],
            recv_sem=x_recv.at[turn, slot],
            device_id=device,
            device_id_type=MESH,
        )

    def y_copy(turn, slot, device):
        return pltpu.make_async_remote_copy(
            src_ref=ys.at[turn],
            dst_ref=yr.at[turn, slot],
            send_sem=y_send.at[turn, slot],
            recv_sem=y_recv.at[turn, slot],
            device_id=device,
            device_id_type=MESH,
        )

    def b_copy(turn, step):
        other = lax.rem(h + step, owners)
        return pltpu.make_async_remote_copy(
            src_ref=bs.at[turn, other],
            dst_ref=br.at[turn, h],
            send_sem=b_send.at[turn, step],
            recv_sem=b_recv.at[turn, step],
            device_id=(r, other),
            device_id_type=MESH,
        )

    def b_arrival(turn, step):
        other = lax.rem(h + owners - step, owners)
        return pltpu.make_async_remote_copy(
            src_ref=bs.at[turn, other],
            dst_ref=br.at[turn, other],
            send_sem=b_send.at[turn, step],
            recv_sem=b_recv.at[turn, step],
            device_id=(r, other),
            device_id_type=MESH,
        )

    def send_rims(turn):
        for copy, dirs in ((x_copy, X_DIRS), (y_copy, Y_DIRS)):
            for slot, direction in enumerate(dirs):
                there, device = target(direction)

                @pl.when(there)
                def _(copy=copy, slot=slot, device=device):
                    copy(turn, slot, device).start()

    def wait_rims(turn):
        for copy, dirs in ((x_copy, X_DIRS), (y_copy, Y_DIRS)):
            for slot, direction in enumerate(dirs):
                there, device = source(direction)

                @pl.when(there)
                def _(copy=copy, slot=slot, device=device):
                    copy(turn, slot, device).wait_recv()

    def wait_sends(turn):
        for copy, dirs in ((x_copy, X_DIRS), (y_copy, Y_DIRS)):
            for slot, direction in enumerate(dirs):
                there, device = target(direction)

                @pl.when(there)
                def _(copy=copy, slot=slot, device=device):
                    copy(turn, slot, device).wait_send()

        for step in range(1, owners):
            b_copy(turn, step).wait_send()

    def put_rims(turn, fields):
        to_next, to_before = pack_x(fields)
        xs[turn][0] = to_next
        xs[turn][1] = to_before
        tiles = pack_y(fields)
        ys[turn, : tiles.shape[0]] = tiles

    def take_rims(turn, count):
        rim_x = unpack_x(xr[turn][0], xr[turn][1])
        column = (iota((1, 8, 128), 2) & 7) < RIM
        before = jnp.where(column, yr[turn, 4], yr[turn, 5])
        beside = jnp.where(column, yr[turn, 2], yr[turn, 3])
        after = jnp.where(column, yr[turn, 0], yr[turn, 1])
        corner = jnp.where(iota((1, 8, 128), 1) < RIM, after, before)
        return rim_x, unpack_y(beside, count), unpack_y(corner, 3 * nz)

    u = load(u_ref)
    lam, mu = load(lam_ref) * (1.0 / 144.0), load(mu_ref) * (1.0 / 144.0)
    put_rims(0, jnp.concatenate([u.reshape(3 * nz, 8, 128), lam, mu], axis=0))
    pl.semaphore_wait(barrier, arrivals)
    send_rims(0)

    cells = load(cells_ref)[0].astype(F32)
    wide = (slots, slots * FOOTPRINT_CELLS)
    own = (iota(wide, 1) // FOOTPRINT_CELLS) == iota(wide, 0)
    corner_cell = jnp.min(jnp.where(own, cells, 1e9), axis=1, keepdims=True)
    corner_x = jnp.floor(corner_cell * (1.0 / 128.0))
    corner_y = corner_cell - 128.0 * corner_x
    lane = iota((slots, 128), 1)
    along_y = lane.astype(F32) - corner_y
    window_y = ((along_y == 0.0) | (along_y == 1.0)).astype(F32).astype(BF16)
    along_x = (lane & 7).astype(F32) - corner_x
    part = lane & 31
    slot_row = iota((slots, 1), 0)
    loads[id(counts_ref)].wait()
    row_counts = counts_ref[0, pl.ds(h, 1), :].astype(F32)
    pairs = (slots, owners)
    live_count = jnp.sum(
        jnp.where(iota(pairs, 0) // capacity == iota(pairs, 1), row_counts, 0.0),
        axis=1,
        keepdims=True,
    )
    live = (slot_row % capacity).astype(F32) < live_count
    weight = jnp.where(
        live & ((along_x == 0.0) | (along_x == 1.0)) & (part < 24), 1.0 / FOOTPRINT_CELLS, 0.0
    )
    square = (slots, slots)
    arch = jnp.sum(
        jnp.where(iota(square, 0) == iota(square, 1), load(arch_ref).astype(F32), 0.0),
        axis=1,
        keepdims=True,
    )
    is_kind = [arch == float(a) for a in range(kinds)]
    couple = load(couple_ref)
    coupling = []
    for c in range(3):
        chosen = jnp.zeros((slots, freedoms), F32)
        for a in range(kinds):
            chosen = jnp.where(is_kind[a], couple[c, a : a + 1, :], chosen)
        coupling.append(chosen)

    def surface_motion(field):
        surface = field[:, 0]
        high = surface.astype(BF16).astype(F32)
        nothing = jnp.zeros((8, 128), F32)
        stacked = jnp.concatenate(
            [high.reshape(24, 128), nothing, (surface - high).reshape(24, 128), nothing]
            + [nothing] * 8,
            axis=0,
        ).astype(BF16)
        gathered = lax.dot_general(
            window_y, stacked, (((1,), (1,)), ((), ())), preferred_element_type=F32
        )
        return gathered * weight

    def base_shear(state):
        shear = [jnp.sum(coupling[c] * state, axis=1, keepdims=True) for c in range(3)]
        return jnp.where(part < 8, shear[0], jnp.where(part < 16, shear[1], shear[2]))

    def send_buildings(turn, field, state):
        both = jnp.where(lane < 64, surface_motion(field), base_shear(state))
        both = both.reshape(owners, capacity, 128)
        bs[turn] = both
        br[turn, h] = bs[turn, h]
        for step in range(1, owners):
            b_copy(turn, step).start()

    def take_buildings(turn):
        for step in range(1, owners):
            b_arrival(turn, step).wait_recv()
        both = br[turn].reshape(slots, 128)
        drive = jnp.zeros((slots, freedoms), F32)
        for c in range(3):
            mine = (lane < 64) & (part >= 8 * c) & (part < 8 * c + 8)
            base = jnp.sum(jnp.where(mine, both, 0.0), axis=1, keepdims=True)
            drive = drive + coupling[c] * base
        pull = both * weight
        high = pull.astype(BF16).astype(F32)
        pull = jnp.where((lane & 32) == 0, high, pull - high)
        spread = lax.dot_general(
            pull.T.astype(BF16), window_y, (((1,), (0,)), ((), ())), preferred_element_type=F32
        )
        force = (spread[64:88] + spread[96:120]).reshape(3, 8, 128)
        return drive, force

    def stiff_term(state):
        high, low = split(state)
        stacked = jnp.concatenate([high.astype(F32), low.astype(F32)], axis=0)
        twice = jnp.concatenate([arch, arch], axis=0)
        spread = jnp.concatenate(
            [jnp.where(twice == float(a), stacked, 0.0).astype(BF16) for a in range(kinds)],
            axis=1,
        )
        product = jnp.dot(spread, table[...], preferred_element_type=F32)
        product = product[:, :freedoms] + product[:, freedoms:]
        return product[:slots] + product[slots:]

    q = load(q_ref)
    send_buildings(0, u, q)
    stiff_high, stiff_low = split(load(stiff_ref).reshape(kinds * freedoms, freedoms))
    table[:, :freedoms] = stiff_high
    table[:, freedoms:] = stiff_low
    stiff = stiff_term(q)
    u_old, q_old = load(u_prev_ref), load(q_prev_ref)
    gain = load(buoy_ref) * (TIME_STEP * TIME_STEP)
    count = 5 * nz
    lam_mu_x = lam_mu_y = None
    for turn in range(STEPS):
        drive, force = take_buildings(turn)
        q, q_old = 2.0 * q - q_old + (TIME_STEP * TIME_STEP) * (drive - stiff), q
        wait_rims(turn)
        rim_x, rim_y, corner = take_rims(turn, count)
        if turn == 0:
            lam_mu_x, lam_mu_y = rim_x[3 * nz :], rim_y[3 * nz :]
        shape = (3, nz, 8, 128)
        total = divergence(
            u,
            rim_x[: 3 * nz].reshape(shape),
            rim_y[: 3 * nz].reshape(shape),
            corner.reshape(shape),
            lam,
            mu,
            lam_mu_x[:nz],
            lam_mu_x[nz:],
            lam_mu_y[:nz],
            lam_mu_y[nz:],
        )
        total = jnp.concatenate([total[:, :1] + force[:, None], total[:, 1:]], axis=1)
        u, u_old = 2.0 * u - u_old + gain * total, u
        count = 3 * nz
        if turn + 1 < STEPS:
            put_rims(turn + 1, u.reshape(3 * nz, 8, 128))
            send_rims(turn + 1)
            send_buildings(turn + 1, u, q)
            u_before_ref[...] = u
            q_before_ref[...] = q
            stiff = stiff_term(q)
    u_last_ref[...] = u
    q_last_ref[...] = q
    for turn in range(STEPS):
        wait_sends(turn)


def shards(
    rows,
    owners,
    u_now,
    u_prev,
    lame_lambda,
    lame_mu,
    buoyancy,
    q_now,
    q_prev,
    archetype,
    stiffness,
    couple,
    counts,
    footprint,
):
    nz = lame_mu.shape[0]
    slots, freedoms = q_now.shape
    capacity = slots // owners
    kinds = stiffness.shape[0]
    pairs = (5 * nz) // 2, (3 * nz) // 2
    vmem = pl.BlockSpec(memory_space=pltpu.VMEM)
    hbm = pl.BlockSpec(memory_space=pltpu.HBM)
    dma = pltpu.SemaphoreType.DMA
    operands = (
        u_now,
        u_prev,
        lame_lambda,
        lame_mu,
        buoyancy,
        q_now,
        q_prev,
        archetype.reshape(1, slots),
        stiffness,
        couple.transpose(1, 0, 2),
        counts,
        footprint,
    )
    results = (
        jax.ShapeDtypeStruct(u_now.shape, F32),
        jax.ShapeDtypeStruct(u_now.shape, F32),
        jax.ShapeDtypeStruct(q_now.shape, F32),
        jax.ShapeDtypeStruct(q_now.shape, F32),
    )
    held = pl.pallas_call(
        functools.partial(kernel, rows, owners),
        out_shape=results,
        in_specs=[hbm] * len(operands),
        out_specs=(vmem,) * 4,
        scratch_shapes=[
            pltpu.VMEM((2, pairs[0], 8, 128), F32),
            pltpu.VMEM((2, pairs[1], 8, 128), F32),
            pltpu.VMEM((2, pairs[0], 8, 128), F32),
            pltpu.VMEM((2, pairs[1], 8, 128), F32),
            pltpu.VMEM((STEPS, 2, 8, 128), F32),
            pltpu.VMEM((STEPS, len(Y_DIRS), 2, 8, 128), F32),
            pltpu.VMEM((STEPS, owners, capacity, 128), F32),
            pltpu.VMEM((STEPS, owners, capacity, 128), F32),
            pltpu.VMEM((kinds * freedoms, 2 * freedoms), BF16),
        ]
        + [pltpu.VMEM(operand.shape, operand.dtype) for operand in operands]
        + [
            dma((len(operands),)),
            dma((STEPS, 2)),
            dma((STEPS, 2)),
            dma((STEPS, len(Y_DIRS))),
            dma((STEPS, len(Y_DIRS))),
            dma((STEPS, owners)),
            dma((STEPS, owners)),
        ],
        compiler_params=pltpu.CompilerParams(
            collective_id=0, has_side_effects=True, vmem_limit_bytes=60 * 1024 * 1024
        ),
    )(*operands)
    return pl.pallas_call(
        store,
        out_shape=results,
        in_specs=[vmem] * 4,
        out_specs=(hbm,) * 4,
        scratch_shapes=[dma((4,))],
    )(*held)


def store(*refs):
    copies = [
        pltpu.make_async_copy(refs[k], refs[4 + k], refs[8].at[k]) for k in range(4)
    ]
    for copy in copies:
        copy.start()
    for copy in copies:
        copy.wait()


def solution(mesh):
    return jax.shard_map(
        functools.partial(shards, mesh.shape["gx"], mesh.shape["gy"]),
        mesh=mesh,
        in_specs=(
            P(None, None, "gx", "gy"),
            P(None, None, "gx", "gy"),
            P(None, "gx", "gy"),
            P(None, "gx", "gy"),
            P(None, "gx", "gy"),
            P(("gx", "gy"), None),
            P(("gx", "gy"), None),
            P(("gx", "gy")),
            P(),
            P(),
            P("gx", None, None),
            P("gx", "gy", None),
        ),
        out_specs=(
            P(None, None, "gx", "gy"),
            P(None, None, "gx", "gy"),
            P(("gx", "gy"), None),
            P(("gx", "gy"), None),
        ),
        check_vma=False,
    )
```

```python
import functools

import jax
import jax.numpy as jnp
from jax import lax
from jax.experimental import pallas as pl
from jax.experimental.pallas import tpu as pltpu
from jax.sharding import PartitionSpec as P

FOOTPRINT_CELLS = 4
STEPS = 2
TIME_STEP = 0.25
RIM = 4
MESH = pl.DeviceIdType.MESH
F32 = jnp.float32
BF16 = jnp.bfloat16

X_DIRS = ((1, 0), (-1, 0))
Y_DIRS = ((-1, 1), (-1, -1), (0, 1), (0, -1), (1, 1), (1, -1))


def iota(shape, dim):
    return lax.broadcasted_iota(jnp.int32, shape, dim)


def split(value):
    high = value.astype(BF16)
    return high, (value - high.astype(F32)).astype(BF16)


def pack_x(fields):
    half = fields.shape[0] // 2
    first, second = fields[:half], fields[half:]
    upper = iota((1, 8, 128), 1) < RIM
    to_next = jnp.where(upper, pltpu.roll(first, RIM, 1), second)
    to_before = jnp.where(upper, first, pltpu.roll(second, RIM, 1))
    return to_next, to_before


def unpack_x(from_before, from_next):
    upper = iota((1, 8, 128), 1) < RIM
    first = jnp.where(upper, from_next, pltpu.roll(from_before, RIM, 1))
    second = jnp.where(upper, pltpu.roll(from_next, RIM, 1), from_before)
    return jnp.concatenate([first, second], axis=0)


def pack_y(fields):
    count = fields.shape[0]
    lane = iota((8, 128), 1)
    tiles = []
    for start in range(0, count, 16):
        tile = jnp.zeros((8, 128), F32)
        for k in range(start, min(start + 16, count)):
            place = 8 * (k - start)
            moved = pltpu.roll(fields[k], (place + RIM) % 128, 1)
            tile = jnp.where((lane >= place) & (lane < place + 8), moved, tile)
        tiles.append(tile)
    return jnp.stack(tiles)


def unpack_y(tiles, count):
    slabs = []
    for k in range(count):
        slabs.append(pltpu.roll(tiles[k // 16], (124 - 8 * (k % 16)) % 128, 1))
    return jnp.stack(slabs)


def slope(here, other, axis, both):
    size = here.shape[axis]
    place = iota((1,) * (here.ndim - 2) + (8, 128), axis)

    def shifted(mine, theirs, shift):
        entering = place < shift if shift > 0 else place >= size + shift
        return pltpu.roll(jnp.where(entering, theirs, mine), (-shift) % size, axis)

    def slope_of(mine, theirs):
        return 8.0 * (shifted(mine, theirs, 1) - shifted(mine, theirs, -1)) - (
            shifted(mine, theirs, 2) - shifted(mine, theirs, -2)
        )

    if both:
        return slope_of(here, other), slope_of(other, here)
    return slope_of(here, other)


def slope_z(field):
    nothing = jnp.zeros((2,) + field.shape[1:], F32)
    padded = jnp.concatenate([nothing, field, nothing], axis=0)
    n = field.shape[0]
    return 8.0 * (padded[3 : n + 3] - padded[1 : n + 1]) - (padded[4 : n + 4] - padded[:n])


def divergence(u, rim_x, rim_y, corner, lam, mu, lam_x, mu_x, lam_y, mu_y):
    ux, uy, uz = u[0], u[1], u[2]
    x_x, x_xh = slope(ux, rim_x[0], 1, True)
    y_x, y_xh = slope(uy, rim_x[1], 1, True)
    z_x, z_xh = slope(uz, rim_x[2], 1, True)
    x_y, x_yh = slope(ux, rim_y[0], 2, True)
    y_y, y_yh = slope(uy, rim_y[1], 2, True)
    z_y, z_yh = slope(uz, rim_y[2], 2, True)
    x_z, y_z, z_z = slope_z(ux), slope_z(uy), slope_z(uz)
    spread = lam * (x_x + y_y + z_z)
    s_xx = spread + 2.0 * mu * x_x
    s_yy = spread + 2.0 * mu * y_y
    s_zz = spread + 2.0 * mu * z_z
    s_xy = mu * (x_y + y_x)
    s_xz = mu * (x_z + z_x)
    s_yz = mu * (y_z + z_y)
    x_yr = slope(rim_x[0], corner[0], 2, False)
    y_yr = slope(rim_x[1], corner[1], 2, False)
    x_zr, z_zr = slope_z(rim_x[0]), slope_z(rim_x[2])
    s_xx_r = lam_x * (x_xh + y_yr + z_zr) + 2.0 * mu_x * x_xh
    s_xy_r = mu_x * (x_yr + y_xh)
    s_xz_r = mu_x * (x_zr + z_xh)
    x_xc = slope(rim_y[0], corner[0], 1, False)
    y_xc = slope(rim_y[1], corner[1], 1, False)
    y_zc, z_zc = slope_z(rim_y[1]), slope_z(rim_y[2])
    s_yy_c = lam_y * (x_xc + y_yh + z_zc) + 2.0 * mu_y * y_yh
    s_xy_c = mu_y * (x_yh + y_xc)
    s_yz_c = mu_y * (y_zc + z_yh)
    total_x = slope(s_xx, s_xx_r, 1, False) + slope(s_xy, s_xy_c, 2, False) + slope_z(s_xz)
    total_y = slope(s_xy, s_xy_r, 1, False) + slope(s_yy, s_yy_c, 2, False) + slope_z(s_yz)
    total_z = slope(s_xz, s_xz_r, 1, False) + slope(s_yz, s_yz_c, 2, False) + slope_z(s_zz)
    return jnp.stack([total_x, total_y, total_z])


def kernel(
    rows,
    owners,
    u_hbm,
    u_prev_hbm,
    lam_hbm,
    mu_hbm,
    buoy_hbm,
    q_hbm,
    q_prev_hbm,
    arch_hbm,
    stiff_hbm,
    couple_hbm,
    counts_hbm,
    cells_hbm,
    u_last_ref,
    u_before_ref,
    q_last_ref,
    q_before_ref,
    xs0,
    xs1,
    xr0,
    xr1,
    ys,
    yr,
    bs,
    br,
    table,
    u_ref,
    u_prev_ref,
    lam_ref,
    mu_ref,
    buoy_ref,
    q_ref,
    q_prev_ref,
    arch_ref,
    stiff_ref,
    couple_ref,
    counts_ref,
    cells_ref,
    loaded,
    x_send,
    x_recv,
    y_send,
    y_recv,
    b_send,
    b_recv,
):
    r, h = lax.axis_index("gx"), lax.axis_index("gy")
    nz = lam_ref.shape[0]
    slots = q_ref.shape[0]
    capacity = slots // owners
    kinds = stiff_ref.shape[0]
    freedoms = q_ref.shape[1]
    xs, xr = (xs0, xs1), (xr0, xr1)

    def target(direction):
        dx, dy = direction
        there = None
        for d, me, n in ((dx, r, rows), (dy, h, owners)):
            if d:
                ok = me + d < n if d > 0 else me > 0
                there = ok if there is None else there & ok
        return there, (r + dx, h + dy)

    def source(direction):
        return target((-direction[0], -direction[1]))

    peers = X_DIRS + tuple(d for d in Y_DIRS if d[0])

    for slot, direction in enumerate(X_DIRS):
        there, _ = source(direction)

        @pl.when(jnp.logical_not(there))
        def _(slot=slot):
            for buffer in xr:
                buffer[slot] = jnp.zeros(buffer.shape[1:], F32)

    for slot, direction in enumerate(Y_DIRS):
        there, _ = source(direction)

        @pl.when(jnp.logical_not(there))
        def _(slot=slot):
            for turn in range(STEPS):
                yr[turn, slot] = jnp.zeros(yr.shape[2:], F32)

    barrier = pltpu.get_barrier_semaphore()
    arrivals = jnp.int32(owners - 1)
    for direction in peers:
        there, device = target(direction)
        arrivals = arrivals + there.astype(jnp.int32)

        @pl.when(there)
        def _(device=device):
            pl.semaphore_signal(barrier, inc=1, device_id=device, device_id_type=MESH)

    for step in range(1, owners):
        other = lax.rem(h + step, owners)
        pl.semaphore_signal(barrier, inc=1, device_id=(r, other), device_id_type=MESH)

    loads = {}
    for source_ref, ref in (
        (u_hbm, u_ref),
        (lam_hbm, lam_ref),
        (mu_hbm, mu_ref),
        (cells_hbm, cells_ref),
        (counts_hbm, counts_ref),
        (q_hbm, q_ref),
        (arch_hbm, arch_ref),
        (couple_hbm, couple_ref),
        (stiff_hbm, stiff_ref),
        (q_prev_hbm, q_prev_ref),
        (u_prev_hbm, u_prev_ref),
        (buoy_hbm, buoy_ref),
    ):
        copy = pltpu.make_async_copy(source_ref, ref, loaded.at[len(loads)])
        copy.start()
        loads[id(ref)] = copy

    def load(ref):
        loads[id(ref)].wait()
        return ref[...]

    def x_copy(turn, slot, device):
        return pltpu.make_async_remote_copy(
            src_ref=xs[turn].at[slot],
            dst_ref=xr[turn].at[slot],
            send_sem=x_send.at[turn, slot],
            recv_sem=x_recv.at[turn, slot],
            device_id=device,
            device_id_type=MESH,
        )

    def y_copy(turn, slot, device):
        return pltpu.make_async_remote_copy(
            src_ref=ys.at[turn],
            dst_ref=yr.at[turn, slot],
            send_sem=y_send.at[turn, slot],
            recv_sem=y_recv.at[turn, slot],
            device_id=device,
            device_id_type=MESH,
        )

    def b_copy(turn, step):
        other = lax.rem(h + step, owners)
        return pltpu.make_async_remote_copy(
            src_ref=bs.at[turn, other],
            dst_ref=br.at[turn, h],
            send_sem=b_send.at[turn, step],
            recv_sem=b_recv.at[turn, step],
            device_id=(r, other),
            device_id_type=MESH,
        )

    def b_arrival(turn, step):
        other = lax.rem(h + owners - step, owners)
        return pltpu.make_async_remote_copy(
            src_ref=bs.at[turn, other],
            dst_ref=br.at[turn, other],
            send_sem=b_send.at[turn, step],
            recv_sem=b_recv.at[turn, step],
            device_id=(r, other),
            device_id_type=MESH,
        )

    def send_rims(turn):
        for copy, dirs in ((x_copy, X_DIRS), (y_copy, Y_DIRS)):
            for slot, direction in enumerate(dirs):
                there, device = target(direction)

                @pl.when(there)
                def _(copy=copy, slot=slot, device=device):
                    copy(turn, slot, device).start()

    def wait_rims(turn):
        for copy, dirs in ((x_copy, X_DIRS), (y_copy, Y_DIRS)):
            for slot, direction in enumerate(dirs):
                there, device = source(direction)

                @pl.when(there)
                def _(copy=copy, slot=slot, device=device):
                    copy(turn, slot, device).wait_recv()

    def wait_sends(turn):
        for copy, dirs in ((x_copy, X_DIRS), (y_copy, Y_DIRS)):
            for slot, direction in enumerate(dirs):
                there, device = target(direction)

                @pl.when(there)
                def _(copy=copy, slot=slot, device=device):
                    copy(turn, slot, device).wait_send()

        for step in range(1, owners):
            b_copy(turn, step).wait_send()

    def put_rims(turn, fields):
        to_next, to_before = pack_x(fields)
        xs[turn][0] = to_next
        xs[turn][1] = to_before
        tiles = pack_y(fields)
        ys[turn, : tiles.shape[0]] = tiles

    def take_rims(turn, count):
        rim_x = unpack_x(xr[turn][0], xr[turn][1])
        column = (iota((1, 8, 128), 2) & 7) < RIM
        before = jnp.where(column, yr[turn, 4], yr[turn, 5])
        beside = jnp.where(column, yr[turn, 2], yr[turn, 3])
        after = jnp.where(column, yr[turn, 0], yr[turn, 1])
        corner = jnp.where(iota((1, 8, 128), 1) < RIM, after, before)
        return rim_x, unpack_y(beside, count), unpack_y(corner, 3 * nz)

    u = load(u_ref)
    lam, mu = load(lam_ref) * (1.0 / 144.0), load(mu_ref) * (1.0 / 144.0)
    put_rims(0, jnp.concatenate([u.reshape(3 * nz, 8, 128), lam, mu], axis=0))
    pl.semaphore_wait(barrier, arrivals)
    send_rims(0)

    cells = load(cells_ref)[0].astype(F32)
    wide = (slots, slots * FOOTPRINT_CELLS)
    own = (iota(wide, 1) // FOOTPRINT_CELLS) == iota(wide, 0)
    corner_cell = jnp.min(jnp.where(own, cells, 1e9), axis=1, keepdims=True)
    corner_x = jnp.floor(corner_cell * (1.0 / 128.0))
    corner_y = corner_cell - 128.0 * corner_x
    lane = iota((slots, 128), 1)
    along_y = lane.astype(F32) - corner_y
    window_y = ((along_y == 0.0) | (along_y == 1.0)).astype(F32).astype(BF16)
    along_x = (lane & 7).astype(F32) - corner_x
    part = lane & 31
    slot_row = iota((slots, 1), 0)
    loads[id(counts_ref)].wait()
    row_counts = counts_ref[0, pl.ds(h, 1), :].astype(F32)
    pairs = (slots, owners)
    live_count = jnp.sum(
        jnp.where(iota(pairs, 0) // capacity == iota(pairs, 1), row_counts, 0.0),
        axis=1,
        keepdims=True,
    )
    live = (slot_row % capacity).astype(F32) < live_count
    weight = jnp.where(
        live & ((along_x == 0.0) | (along_x == 1.0)) & (part < 24), 1.0 / FOOTPRINT_CELLS, 0.0
    )
    square = (slots, slots)
    arch = jnp.sum(
        jnp.where(iota(square, 0) == iota(square, 1), load(arch_ref).astype(F32), 0.0),
        axis=1,
        keepdims=True,
    )
    is_kind = [arch == float(a) for a in range(kinds)]
    couple = load(couple_ref)
    coupling = []
    for c in range(3):
        chosen = jnp.zeros((slots, freedoms), F32)
        for a in range(kinds):
            chosen = jnp.where(is_kind[a], couple[c, a : a + 1, :], chosen)
        coupling.append(chosen)

    def surface_motion(field):
        surface = field[:, 0]
        high = surface.astype(BF16).astype(F32)
        nothing = jnp.zeros((8, 128), F32)
        stacked = jnp.concatenate(
            [high.reshape(24, 128), nothing, (surface - high).reshape(24, 128), nothing]
            + [nothing] * 8,
            axis=0,
        ).astype(BF16)
        gathered = lax.dot_general(
            window_y, stacked, (((1,), (1,)), ((), ())), preferred_element_type=F32
        )
        return gathered * weight

    def base_shear(state):
        shear = [jnp.sum(coupling[c] * state, axis=1, keepdims=True) for c in range(3)]
        return jnp.where(part < 8, shear[0], jnp.where(part < 16, shear[1], shear[2]))

    def send_buildings(turn, field, state):
        both = jnp.where(lane < 64, surface_motion(field), base_shear(state))
        both = both.reshape(owners, capacity, 128)
        bs[turn] = both
        br[turn, h] = bs[turn, h]
        for step in range(1, owners):
            b_copy(turn, step).start()

    def take_buildings(turn):
        for step in range(1, owners):
            b_arrival(turn, step).wait_recv()
        both = br[turn].reshape(slots, 128)
        drive = jnp.zeros((slots, freedoms), F32)
        for c in range(3):
            mine = (lane < 64) & (part >= 8 * c) & (part < 8 * c + 8)
            base = jnp.sum(jnp.where(mine, both, 0.0), axis=1, keepdims=True)
            drive = drive + coupling[c] * base
        pull = both * weight
        high = pull.astype(BF16).astype(F32)
        pull = jnp.where((lane & 32) == 0, high, pull - high)
        spread = lax.dot_general(
            pull.T.astype(BF16), window_y, (((1,), (0,)), ((), ())), preferred_element_type=F32
        )
        force = (spread[64:88] + spread[96:120]).reshape(3, 8, 128)
        return drive, force

    def stiff_term(state):
        high, low = split(state)
        stacked = jnp.concatenate([high.astype(F32), low.astype(F32)], axis=0)
        twice = jnp.concatenate([arch, arch], axis=0)
        spread = jnp.concatenate(
            [jnp.where(twice == float(a), stacked, 0.0).astype(BF16) for a in range(kinds)],
            axis=1,
        )
        product = jnp.dot(spread, table[...], preferred_element_type=F32)
        product = product[:, :freedoms] + product[:, freedoms:]
        return product[:slots] + product[slots:]

    q = load(q_ref)
    send_buildings(0, u, q)
    stiff_high, stiff_low = split(load(stiff_ref).reshape(kinds * freedoms, freedoms))
    table[:, :freedoms] = stiff_high
    table[:, freedoms:] = stiff_low
    stiff = stiff_term(q)
    u_old, q_old = load(u_prev_ref), load(q_prev_ref)
    gain = load(buoy_ref) * (TIME_STEP * TIME_STEP)
    count = 5 * nz
    lam_mu_x = lam_mu_y = None
    for turn in range(STEPS):
        drive, force = take_buildings(turn)
        q, q_old = 2.0 * q - q_old + (TIME_STEP * TIME_STEP) * (drive - stiff), q
        wait_rims(turn)
        rim_x, rim_y, corner = take_rims(turn, count)
        if turn == 0:
            lam_mu_x, lam_mu_y = rim_x[3 * nz :], rim_y[3 * nz :]
        shape = (3, nz, 8, 128)
        total = divergence(
            u,
            rim_x[: 3 * nz].reshape(shape),
            rim_y[: 3 * nz].reshape(shape),
            corner.reshape(shape),
            lam,
            mu,
            lam_mu_x[:nz],
            lam_mu_x[nz:],
            lam_mu_y[:nz],
            lam_mu_y[nz:],
        )
        total = jnp.concatenate([total[:, :1] + force[:, None], total[:, 1:]], axis=1)
        u, u_old = 2.0 * u - u_old + gain * total, u
        count = 3 * nz
        if turn + 1 < STEPS:
            put_rims(turn + 1, u.reshape(3 * nz, 8, 128))
            send_rims(turn + 1)
            send_buildings(turn + 1, u, q)
            u_before_ref[...] = u
            q_before_ref[...] = q
            stiff = stiff_term(q)
    u_last_ref[...] = u
    q_last_ref[...] = q
    for turn in range(STEPS):
        wait_sends(turn)


def shards(
    rows,
    owners,
    u_now,
    u_prev,
    lame_lambda,
    lame_mu,
    buoyancy,
    q_now,
    q_prev,
    archetype,
    stiffness,
    couple,
    counts,
    footprint,
):
    nz = lame_mu.shape[0]
    slots, freedoms = q_now.shape
    capacity = slots // owners
    kinds = stiffness.shape[0]
    pairs = (5 * nz) // 2, (3 * nz) // 2
    vmem = pl.BlockSpec(memory_space=pltpu.VMEM)
    hbm = pl.BlockSpec(memory_space=pltpu.HBM)
    dma = pltpu.SemaphoreType.DMA
    operands = (
        u_now,
        u_prev,
        lame_lambda,
        lame_mu,
        buoyancy,
        q_now,
        q_prev,
        archetype.reshape(1, slots),
        stiffness,
        couple.transpose(1, 0, 2),
        counts,
        footprint,
    )
    results = (
        jax.ShapeDtypeStruct(u_now.shape, F32),
        jax.ShapeDtypeStruct(u_now.shape, F32),
        jax.ShapeDtypeStruct(q_now.shape, F32),
        jax.ShapeDtypeStruct(q_now.shape, F32),
    )
    held = pl.pallas_call(
        functools.partial(kernel, rows, owners),
        out_shape=tuple(pltpu.VMEM(result.shape, result.dtype) for result in results),
        in_specs=[hbm] * len(operands),
        out_specs=(vmem,) * 4,
        scratch_shapes=[
            pltpu.VMEM((2, pairs[0], 8, 128), F32),
            pltpu.VMEM((2, pairs[1], 8, 128), F32),
            pltpu.VMEM((2, pairs[0], 8, 128), F32),
            pltpu.VMEM((2, pairs[1], 8, 128), F32),
            pltpu.VMEM((STEPS, 2, 8, 128), F32),
            pltpu.VMEM((STEPS, len(Y_DIRS), 2, 8, 128), F32),
            pltpu.VMEM((STEPS, owners, capacity, 128), F32),
            pltpu.VMEM((STEPS, owners, capacity, 128), F32),
            pltpu.VMEM((kinds * freedoms, 2 * freedoms), BF16),
        ]
        + [pltpu.VMEM(operand.shape, operand.dtype) for operand in operands]
        + [
            dma((len(operands),)),
            dma((STEPS, 2)),
            dma((STEPS, 2)),
            dma((STEPS, len(Y_DIRS))),
            dma((STEPS, len(Y_DIRS))),
            dma((STEPS, owners)),
            dma((STEPS, owners)),
        ],
        compiler_params=pltpu.CompilerParams(
            collective_id=0, has_side_effects=True, vmem_limit_bytes=60 * 1024 * 1024
        ),
    )(*operands)
    return pl.pallas_call(
        store,
        out_shape=results,
        in_specs=[vmem] * 4,
        out_specs=(hbm,) * 4,
        scratch_shapes=[dma((4,))],
        compiler_params=pltpu.CompilerParams(vmem_limit_bytes=1024 * 1024),
    )(*held)


def store(*refs):
    copies = [
        pltpu.make_async_copy(refs[k], refs[4 + k], refs[8].at[k]) for k in range(4)
    ]
    for copy in copies:
        copy.start()
    for copy in copies:
        copy.wait()


def solution(mesh):
    return jax.shard_map(
        functools.partial(shards, mesh.shape["gx"], mesh.shape["gy"]),
        mesh=mesh,
        in_specs=(
            P(None, None, "gx", "gy"),
            P(None, None, "gx", "gy"),
            P(None, "gx", "gy"),
            P(None, "gx", "gy"),
            P(None, "gx", "gy"),
            P(("gx", "gy"), None),
            P(("gx", "gy"), None),
            P(("gx", "gy")),
            P(),
            P(),
            P("gx", None, None),
            P("gx", "gy", None),
        ),
        out_specs=(
            P(None, None, "gx", "gy"),
            P(None, None, "gx", "gy"),
            P(("gx", "gy"), None),
            P(("gx", "gy"), None),
        ),
        check_vma=False,
    )
```

```python
import functools

import jax
import jax.numpy as jnp
from jax import lax
from jax.experimental import pallas as pl
from jax.experimental.pallas import tpu as pltpu
from jax.sharding import PartitionSpec as P

FOOTPRINT_CELLS = 4
STEPS = 2
TIME_STEP = 0.25
RIM = 4
MESH = pl.DeviceIdType.MESH
F32 = jnp.float32
BF16 = jnp.bfloat16

X_DIRS = ((1, 0), (-1, 0))
Y_DIRS = ((-1, 1), (-1, -1), (0, 1), (0, -1), (1, 1), (1, -1))


def iota(shape, dim):
    return lax.broadcasted_iota(jnp.int32, shape, dim)


def split(value):
    high = value.astype(BF16)
    return high, (value - high.astype(F32)).astype(BF16)


def pack_x(fields):
    half = fields.shape[0] // 2
    first, second = fields[:half], fields[half:]
    upper = iota((1, 8, 128), 1) < RIM
    to_next = jnp.where(upper, pltpu.roll(first, RIM, 1), second)
    to_before = jnp.where(upper, first, pltpu.roll(second, RIM, 1))
    return to_next, to_before


def unpack_x(from_before, from_next):
    upper = iota((1, 8, 128), 1) < RIM
    first = jnp.where(upper, from_next, pltpu.roll(from_before, RIM, 1))
    second = jnp.where(upper, pltpu.roll(from_next, RIM, 1), from_before)
    return jnp.concatenate([first, second], axis=0)


def pack_y(fields):
    count = fields.shape[0]
    lane = iota((8, 128), 1)
    tiles = []
    for start in range(0, count, 16):
        tile = jnp.zeros((8, 128), F32)
        for k in range(start, min(start + 16, count)):
            place = 8 * (k - start)
            moved = pltpu.roll(fields[k], (place + RIM) % 128, 1)
            tile = jnp.where((lane >= place) & (lane < place + 8), moved, tile)
        tiles.append(tile)
    return jnp.stack(tiles)


def unpack_y(tiles, count):
    slabs = []
    for k in range(count):
        slabs.append(pltpu.roll(tiles[k // 16], (124 - 8 * (k % 16)) % 128, 1))
    return jnp.stack(slabs)


def slope(here, other, axis, both):
    size = here.shape[axis]
    place = iota((1,) * (here.ndim - 2) + (8, 128), axis)

    def shifted(mine, theirs, shift):
        entering = place < shift if shift > 0 else place >= size + shift
        return pltpu.roll(jnp.where(entering, theirs, mine), (-shift) % size, axis)

    def slope_of(mine, theirs):
        return 8.0 * (shifted(mine, theirs, 1) - shifted(mine, theirs, -1)) - (
            shifted(mine, theirs, 2) - shifted(mine, theirs, -2)
        )

    if both:
        return slope_of(here, other), slope_of(other, here)
    return slope_of(here, other)


def slope_z(field):
    nothing = jnp.zeros((2,) + field.shape[1:], F32)
    padded = jnp.concatenate([nothing, field, nothing], axis=0)
    n = field.shape[0]
    return 8.0 * (padded[3 : n + 3] - padded[1 : n + 1]) - (padded[4 : n + 4] - padded[:n])


def divergence(u, rim_x, rim_y, corner, lam, mu, lam_x, mu_x, lam_y, mu_y):
    ux, uy, uz = u[0], u[1], u[2]
    x_x, x_xh = slope(ux, rim_x[0], 1, True)
    y_x, y_xh = slope(uy, rim_x[1], 1, True)
    z_x, z_xh = slope(uz, rim_x[2], 1, True)
    x_y, x_yh = slope(ux, rim_y[0], 2, True)
    y_y, y_yh = slope(uy, rim_y[1], 2, True)
    z_y, z_yh = slope(uz, rim_y[2], 2, True)
    x_z, y_z, z_z = slope_z(ux), slope_z(uy), slope_z(uz)
    spread = lam * (x_x + y_y + z_z)
    s_xx = spread + 2.0 * mu * x_x
    s_yy = spread + 2.0 * mu * y_y
    s_zz = spread + 2.0 * mu * z_z
    s_xy = mu * (x_y + y_x)
    s_xz = mu * (x_z + z_x)
    s_yz = mu * (y_z + z_y)
    x_yr = slope(rim_x[0], corner[0], 2, False)
    y_yr = slope(rim_x[1], corner[1], 2, False)
    x_zr, z_zr = slope_z(rim_x[0]), slope_z(rim_x[2])
    s_xx_r = lam_x * (x_xh + y_yr + z_zr) + 2.0 * mu_x * x_xh
    s_xy_r = mu_x * (x_yr + y_xh)
    s_xz_r = mu_x * (x_zr + z_xh)
    x_xc = slope(rim_y[0], corner[0], 1, False)
    y_xc = slope(rim_y[1], corner[1], 1, False)
    y_zc, z_zc = slope_z(rim_y[1]), slope_z(rim_y[2])
    s_yy_c = lam_y * (x_xc + y_yh + z_zc) + 2.0 * mu_y * y_yh
    s_xy_c = mu_y * (x_yh + y_xc)
    s_yz_c = mu_y * (y_zc + z_yh)
    total_x = slope(s_xx, s_xx_r, 1, False) + slope(s_xy, s_xy_c, 2, False) + slope_z(s_xz)
    total_y = slope(s_xy, s_xy_r, 1, False) + slope(s_yy, s_yy_c, 2, False) + slope_z(s_yz)
    total_z = slope(s_xz, s_xz_r, 1, False) + slope(s_yz, s_yz_c, 2, False) + slope_z(s_zz)
    return jnp.stack([total_x, total_y, total_z])


def kernel(
    rows,
    owners,
    u_hbm,
    u_prev_hbm,
    lam_hbm,
    mu_hbm,
    buoy_hbm,
    q_hbm,
    q_prev_hbm,
    arch_hbm,
    stiff_hbm,
    couple_hbm,
    counts_hbm,
    cells_hbm,
    u_last_ref,
    u_before_ref,
    q_last_ref,
    q_before_ref,
    xs0,
    xs1,
    xr0,
    xr1,
    ys,
    yr,
    bs,
    br,
    table,
    u_ref,
    u_prev_ref,
    lam_ref,
    mu_ref,
    buoy_ref,
    q_ref,
    q_prev_ref,
    arch_ref,
    stiff_ref,
    couple_ref,
    counts_ref,
    cells_ref,
    loaded,
    x_send,
    x_recv,
    y_send,
    y_recv,
    b_send,
    b_recv,
):
    r, h = lax.axis_index("gx"), lax.axis_index("gy")
    nz = lam_ref.shape[0]
    slots = q_ref.shape[0]
    capacity = slots // owners
    kinds = stiff_ref.shape[0]
    freedoms = q_ref.shape[1]
    xs, xr = (xs0, xs1), (xr0, xr1)

    def target(direction):
        dx, dy = direction
        there = None
        for d, me, n in ((dx, r, rows), (dy, h, owners)):
            if d:
                ok = me + d < n if d > 0 else me > 0
                there = ok if there is None else there & ok
        return there, (r + dx, h + dy)

    def source(direction):
        return target((-direction[0], -direction[1]))

    peers = X_DIRS + tuple(d for d in Y_DIRS if d[0])

    for slot, direction in enumerate(X_DIRS):
        there, _ = source(direction)

        @pl.when(jnp.logical_not(there))
        def _(slot=slot):
            for buffer in xr:
                buffer[slot] = jnp.zeros(buffer.shape[1:], F32)

    for slot, direction in enumerate(Y_DIRS):
        there, _ = source(direction)

        @pl.when(jnp.logical_not(there))
        def _(slot=slot):
            for turn in range(STEPS):
                yr[turn, slot] = jnp.zeros(yr.shape[2:], F32)

    barrier = pltpu.get_barrier_semaphore()
    arrivals = jnp.int32(owners - 1)
    for direction in peers:
        there, device = target(direction)
        arrivals = arrivals + there.astype(jnp.int32)

        @pl.when(there)
        def _(device=device):
            pl.semaphore_signal(barrier, inc=1, device_id=device, device_id_type=MESH)

    for step in range(1, owners):
        other = lax.rem(h + step, owners)
        pl.semaphore_signal(barrier, inc=1, device_id=(r, other), device_id_type=MESH)

    loads = {}
    for source_ref, ref in (
        (cells_hbm, cells_ref),
        (counts_hbm, counts_ref),
        (arch_hbm, arch_ref),
        (couple_hbm, couple_ref),
        (u_hbm, u_ref),
        (q_hbm, q_ref),
        (lam_hbm, lam_ref),
        (mu_hbm, mu_ref),
        (stiff_hbm, stiff_ref),
        (q_prev_hbm, q_prev_ref),
        (u_prev_hbm, u_prev_ref),
        (buoy_hbm, buoy_ref),
    ):
        copy = pltpu.make_async_copy(source_ref, ref, loaded.at[len(loads)])
        copy.start()
        loads[id(ref)] = copy

    def load(ref):
        loads[id(ref)].wait()
        return ref[...]

    def x_copy(turn, slot, device):
        return pltpu.make_async_remote_copy(
            src_ref=xs[turn].at[slot],
            dst_ref=xr[turn].at[slot],
            send_sem=x_send.at[turn, slot],
            recv_sem=x_recv.at[turn, slot],
            device_id=device,
            device_id_type=MESH,
        )

    def y_copy(turn, slot, device):
        return pltpu.make_async_remote_copy(
            src_ref=ys.at[turn],
            dst_ref=yr.at[turn, slot],
            send_sem=y_send.at[turn, slot],
            recv_sem=y_recv.at[turn, slot],
            device_id=device,
            device_id_type=MESH,
        )

    def b_copy(turn, step):
        other = lax.rem(h + step, owners)
        return pltpu.make_async_remote_copy(
            src_ref=bs.at[turn, other],
            dst_ref=br.at[turn, h],
            send_sem=b_send.at[turn, step],
            recv_sem=b_recv.at[turn, step],
            device_id=(r, other),
            device_id_type=MESH,
        )

    def b_arrival(turn, step):
        other = lax.rem(h + owners - step, owners)
        return pltpu.make_async_remote_copy(
            src_ref=bs.at[turn, other],
            dst_ref=br.at[turn, other],
            send_sem=b_send.at[turn, step],
            recv_sem=b_recv.at[turn, step],
            device_id=(r, other),
            device_id_type=MESH,
        )

    def send_rims(turn):
        for copy, dirs in ((x_copy, X_DIRS), (y_copy, Y_DIRS)):
            for slot, direction in enumerate(dirs):
                there, device = target(direction)

                @pl.when(there)
                def _(copy=copy, slot=slot, device=device):
                    copy(turn, slot, device).start()

    def wait_rims(turn):
        for copy, dirs in ((x_copy, X_DIRS), (y_copy, Y_DIRS)):
            for slot, direction in enumerate(dirs):
                there, device = source(direction)

                @pl.when(there)
                def _(copy=copy, slot=slot, device=device):
                    copy(turn, slot, device).wait_recv()

    def wait_sends(turn):
        for copy, dirs in ((x_copy, X_DIRS), (y_copy, Y_DIRS)):
            for slot, direction in enumerate(dirs):
                there, device = target(direction)

                @pl.when(there)
                def _(copy=copy, slot=slot, device=device):
                    copy(turn, slot, device).wait_send()

        for step in range(1, owners):
            b_copy(turn, step).wait_send()

    def put_rims(turn, fields):
        to_next, to_before = pack_x(fields)
        xs[turn][0] = to_next
        xs[turn][1] = to_before
        tiles = pack_y(fields)
        ys[turn, : tiles.shape[0]] = tiles

    def take_rims(turn, count):
        rim_x = unpack_x(xr[turn][0], xr[turn][1])
        column = (iota((1, 8, 128), 2) & 7) < RIM
        before = jnp.where(column, yr[turn, 4], yr[turn, 5])
        beside = jnp.where(column, yr[turn, 2], yr[turn, 3])
        after = jnp.where(column, yr[turn, 0], yr[turn, 1])
        corner = jnp.where(iota((1, 8, 128), 1) < RIM, after, before)
        return rim_x, unpack_y(beside, count), unpack_y(corner, 3 * nz)


    cells = load(cells_ref)[0].astype(F32)
    wide = (slots, slots * FOOTPRINT_CELLS)
    own = (iota(wide, 1) // FOOTPRINT_CELLS) == iota(wide, 0)
    corner_cell = jnp.min(jnp.where(own, cells, 1e9), axis=1, keepdims=True)
    corner_x = jnp.floor(corner_cell * (1.0 / 128.0))
    corner_y = corner_cell - 128.0 * corner_x
    lane = iota((slots, 128), 1)
    along_y = lane.astype(F32) - corner_y
    window_y = ((along_y == 0.0) | (along_y == 1.0)).astype(F32).astype(BF16)
    along_x = (lane & 7).astype(F32) - corner_x
    part = lane & 31
    slot_row = iota((slots, 1), 0)
    loads[id(counts_ref)].wait()
    row_counts = counts_ref[0, pl.ds(h, 1), :].astype(F32)
    pairs = (slots, owners)
    live_count = jnp.sum(
        jnp.where(iota(pairs, 0) // capacity == iota(pairs, 1), row_counts, 0.0),
        axis=1,
        keepdims=True,
    )
    live = (slot_row % capacity).astype(F32) < live_count
    weight = jnp.where(
        live & ((along_x == 0.0) | (along_x == 1.0)) & (part < 24), 1.0 / FOOTPRINT_CELLS, 0.0
    )
    square = (slots, slots)
    arch = jnp.sum(
        jnp.where(iota(square, 0) == iota(square, 1), load(arch_ref).astype(F32), 0.0),
        axis=1,
        keepdims=True,
    )
    is_kind = [arch == float(a) for a in range(kinds)]
    couple = load(couple_ref)
    coupling = []
    for c in range(3):
        chosen = jnp.zeros((slots, freedoms), F32)
        for a in range(kinds):
            chosen = jnp.where(is_kind[a], couple[c, a : a + 1, :], chosen)
        coupling.append(chosen)

    def surface_motion(field):
        surface = field[:, 0]
        high = surface.astype(BF16).astype(F32)
        nothing = jnp.zeros((8, 128), F32)
        stacked = jnp.concatenate(
            [high.reshape(24, 128), nothing, (surface - high).reshape(24, 128), nothing]
            + [nothing] * 8,
            axis=0,
        ).astype(BF16)
        gathered = lax.dot_general(
            window_y, stacked, (((1,), (1,)), ((), ())), preferred_element_type=F32
        )
        return gathered * weight

    def base_shear(state):
        shear = [jnp.sum(coupling[c] * state, axis=1, keepdims=True) for c in range(3)]
        return jnp.where(part < 8, shear[0], jnp.where(part < 16, shear[1], shear[2]))

    def put_buildings(turn, field, state):
        both = jnp.where(lane < 64, surface_motion(field), base_shear(state))
        both = both.reshape(owners, capacity, 128)
        bs[turn] = both
        br[turn, h] = bs[turn, h]

    def send_buildings(turn):
        for step in range(owners // 2, 0, -1):
            b_copy(turn, step).start()
            if owners - step != step:
                b_copy(turn, owners - step).start()

    def take_buildings(turn):
        for step in range(1, owners):
            b_arrival(turn, step).wait_recv()
        both = br[turn].reshape(slots, 128)
        drive = jnp.zeros((slots, freedoms), F32)
        for c in range(3):
            mine = (lane < 64) & (part >= 8 * c) & (part < 8 * c + 8)
            base = jnp.sum(jnp.where(mine, both, 0.0), axis=1, keepdims=True)
            drive = drive + coupling[c] * base
        pull = both * weight
        high = pull.astype(BF16).astype(F32)
        pull = jnp.where((lane & 32) == 0, high, pull - high)
        spread = lax.dot_general(
            pull.T.astype(BF16), window_y, (((1,), (0,)), ((), ())), preferred_element_type=F32
        )
        force = (spread[64:88] + spread[96:120]).reshape(3, 8, 128)
        return drive, force

    def stiff_term(state):
        high, low = split(state)
        stacked = jnp.concatenate([high.astype(F32), low.astype(F32)], axis=0)
        twice = jnp.concatenate([arch, arch], axis=0)
        spread = jnp.concatenate(
            [jnp.where(twice == float(a), stacked, 0.0).astype(BF16) for a in range(kinds)],
            axis=1,
        )
        product = jnp.dot(spread, table[...], preferred_element_type=F32)
        product = product[:, :freedoms] + product[:, freedoms:]
        return product[:slots] + product[slots:]

    u, q = load(u_ref), load(q_ref)
    put_buildings(0, u, q)
    lam, mu = load(lam_ref) * (1.0 / 144.0), load(mu_ref) * (1.0 / 144.0)
    put_rims(0, jnp.concatenate([u.reshape(3 * nz, 8, 128), lam, mu], axis=0))
    pl.semaphore_wait(barrier, arrivals)
    send_buildings(0)
    send_rims(0)
    stiff_high, stiff_low = split(load(stiff_ref).reshape(kinds * freedoms, freedoms))
    table[:, :freedoms] = stiff_high
    table[:, freedoms:] = stiff_low
    stiff = stiff_term(q)
    u_old, q_old = load(u_prev_ref), load(q_prev_ref)
    gain = load(buoy_ref) * (TIME_STEP * TIME_STEP)
    count = 5 * nz
    lam_mu_x = lam_mu_y = None
    for turn in range(STEPS):
        wait_rims(turn)
        rim_x, rim_y, corner = take_rims(turn, count)
        if turn == 0:
            lam_mu_x, lam_mu_y = rim_x[3 * nz :], rim_y[3 * nz :]
        shape = (3, nz, 8, 128)
        total = divergence(
            u,
            rim_x[: 3 * nz].reshape(shape),
            rim_y[: 3 * nz].reshape(shape),
            corner.reshape(shape),
            lam,
            mu,
            lam_mu_x[:nz],
            lam_mu_x[nz:],
            lam_mu_y[:nz],
            lam_mu_y[nz:],
        )
        drive, force = take_buildings(turn)
        q, q_old = 2.0 * q - q_old + (TIME_STEP * TIME_STEP) * (drive - stiff), q
        total = jnp.concatenate([total[:, :1] + force[:, None], total[:, 1:]], axis=1)
        u, u_old = 2.0 * u - u_old + gain * total, u
        count = 3 * nz
        if turn + 1 < STEPS:
            put_buildings(turn + 1, u, q)
            send_buildings(turn + 1)
            put_rims(turn + 1, u.reshape(3 * nz, 8, 128))
            send_rims(turn + 1)
            u_before_ref[...] = u
            q_before_ref[...] = q
            stiff = stiff_term(q)
    u_last_ref[...] = u
    q_last_ref[...] = q
    for turn in range(STEPS):
        wait_sends(turn)


def shards(
    rows,
    owners,
    u_now,
    u_prev,
    lame_lambda,
    lame_mu,
    buoyancy,
    q_now,
    q_prev,
    archetype,
    stiffness,
    couple,
    counts,
    footprint,
):
    nz = lame_mu.shape[0]
    slots, freedoms = q_now.shape
    capacity = slots // owners
    kinds = stiffness.shape[0]
    pairs = (5 * nz) // 2, (3 * nz) // 2
    vmem = pl.BlockSpec(memory_space=pltpu.VMEM)
    hbm = pl.BlockSpec(memory_space=pltpu.HBM)
    dma = pltpu.SemaphoreType.DMA
    operands = (
        u_now,
        u_prev,
        lame_lambda,
        lame_mu,
        buoyancy,
        q_now,
        q_prev,
        archetype.reshape(1, slots),
        stiffness,
        couple.transpose(1, 0, 2),
        counts,
        footprint,
    )
    results = (
        jax.ShapeDtypeStruct(u_now.shape, F32),
        jax.ShapeDtypeStruct(u_now.shape, F32),
        jax.ShapeDtypeStruct(q_now.shape, F32),
        jax.ShapeDtypeStruct(q_now.shape, F32),
    )
    held = pl.pallas_call(
        functools.partial(kernel, rows, owners),
        out_shape=tuple(pltpu.VMEM(result.shape, result.dtype) for result in results),
        in_specs=[hbm] * len(operands),
        out_specs=(vmem,) * 4,
        scratch_shapes=[
            pltpu.VMEM((2, pairs[0], 8, 128), F32),
            pltpu.VMEM((2, pairs[1], 8, 128), F32),
            pltpu.VMEM((2, pairs[0], 8, 128), F32),
            pltpu.VMEM((2, pairs[1], 8, 128), F32),
            pltpu.VMEM((STEPS, 2, 8, 128), F32),
            pltpu.VMEM((STEPS, len(Y_DIRS), 2, 8, 128), F32),
            pltpu.VMEM((STEPS, owners, capacity, 128), F32),
            pltpu.VMEM((STEPS, owners, capacity, 128), F32),
            pltpu.VMEM((kinds * freedoms, 2 * freedoms), BF16),
        ]
        + [pltpu.VMEM(operand.shape, operand.dtype) for operand in operands]
        + [
            dma((len(operands),)),
            dma((STEPS, 2)),
            dma((STEPS, 2)),
            dma((STEPS, len(Y_DIRS))),
            dma((STEPS, len(Y_DIRS))),
            dma((STEPS, owners)),
            dma((STEPS, owners)),
        ],
        compiler_params=pltpu.CompilerParams(
            collective_id=0, has_side_effects=True, vmem_limit_bytes=60 * 1024 * 1024
        ),
    )(*operands)
    return pl.pallas_call(
        store,
        out_shape=results,
        in_specs=[vmem] * 4,
        out_specs=(hbm,) * 4,
        scratch_shapes=[dma((4,))],
        compiler_params=pltpu.CompilerParams(vmem_limit_bytes=1024 * 1024),
    )(*held)


def store(*refs):
    copies = [
        pltpu.make_async_copy(refs[k], refs[4 + k], refs[8].at[k]) for k in range(4)
    ]
    for copy in copies:
        copy.start()
    for copy in copies:
        copy.wait()


def solution(mesh):
    return jax.shard_map(
        functools.partial(shards, mesh.shape["gx"], mesh.shape["gy"]),
        mesh=mesh,
        in_specs=(
            P(None, None, "gx", "gy"),
            P(None, None, "gx", "gy"),
            P(None, "gx", "gy"),
            P(None, "gx", "gy"),
            P(None, "gx", "gy"),
            P(("gx", "gy"), None),
            P(("gx", "gy"), None),
            P(("gx", "gy")),
            P(),
            P(),
            P("gx", None, None),
            P("gx", "gy", None),
        ),
        out_specs=(
            P(None, None, "gx", "gy"),
            P(None, None, "gx", "gy"),
            P(("gx", "gy"), None),
            P(("gx", "gy"), None),
        ),
        check_vma=False,
    )
```

```python
import functools

import jax
import jax.numpy as jnp
from jax import lax
from jax.experimental import pallas as pl
from jax.experimental.pallas import tpu as pltpu
from jax.sharding import PartitionSpec as P

FOOTPRINT_CELLS = 4
STEPS = 2
TIME_STEP = 0.25
RIM = 4
MESH = pl.DeviceIdType.MESH
F32 = jnp.float32
BF16 = jnp.bfloat16

X_DIRS = ((1, 0), (-1, 0))
Y_DIRS = ((-1, 1), (-1, -1), (0, 1), (0, -1), (1, 1), (1, -1))


def iota(shape, dim):
    return lax.broadcasted_iota(jnp.int32, shape, dim)


def split(value):
    high = value.astype(BF16)
    return high, (value - high.astype(F32)).astype(BF16)


def pack_x(fields):
    half = fields.shape[0] // 2
    first, second = fields[:half], fields[half:]
    upper = iota((1, 8, 128), 1) < RIM
    to_next = jnp.where(upper, pltpu.roll(first, RIM, 1), second)
    to_before = jnp.where(upper, first, pltpu.roll(second, RIM, 1))
    return to_next, to_before


def unpack_x(from_before, from_next):
    upper = iota((1, 8, 128), 1) < RIM
    first = jnp.where(upper, from_next, pltpu.roll(from_before, RIM, 1))
    second = jnp.where(upper, pltpu.roll(from_next, RIM, 1), from_before)
    return jnp.concatenate([first, second], axis=0)


def pack_y(fields):
    count = fields.shape[0]
    lane = iota((8, 128), 1)
    tiles = []
    for start in range(0, count, 16):
        tile = jnp.zeros((8, 128), F32)
        for k in range(start, min(start + 16, count)):
            place = 8 * (k - start)
            moved = pltpu.roll(fields[k], (place + RIM) % 128, 1)
            tile = jnp.where((lane >= place) & (lane < place + 8), moved, tile)
        tiles.append(tile)
    return jnp.stack(tiles)


def unpack_y(tiles, count):
    slabs = []
    for k in range(count):
        slabs.append(pltpu.roll(tiles[k // 16], (124 - 8 * (k % 16)) % 128, 1))
    return jnp.stack(slabs)


def slope(here, other, axis, both):
    size = here.shape[axis]
    place = iota((1,) * (here.ndim - 2) + (8, 128), axis)

    def shifted(mine, theirs, shift):
        entering = place < shift if shift > 0 else place >= size + shift
        return pltpu.roll(jnp.where(entering, theirs, mine), (-shift) % size, axis)

    def slope_of(mine, theirs):
        return 8.0 * (shifted(mine, theirs, 1) - shifted(mine, theirs, -1)) - (
            shifted(mine, theirs, 2) - shifted(mine, theirs, -2)
        )

    if both:
        return slope_of(here, other), slope_of(other, here)
    return slope_of(here, other)


def slope_z(field):
    nothing = jnp.zeros((2,) + field.shape[1:], F32)
    padded = jnp.concatenate([nothing, field, nothing], axis=0)
    n = field.shape[0]
    return 8.0 * (padded[3 : n + 3] - padded[1 : n + 1]) - (padded[4 : n + 4] - padded[:n])


def divergence(u, rim_x, rim_y, corner, lam, mu, lam_x, mu_x, lam_y, mu_y):
    ux, uy, uz = u[0], u[1], u[2]
    x_x, x_xh = slope(ux, rim_x[0], 1, True)
    y_x, y_xh = slope(uy, rim_x[1], 1, True)
    z_x, z_xh = slope(uz, rim_x[2], 1, True)
    x_y, x_yh = slope(ux, rim_y[0], 2, True)
    y_y, y_yh = slope(uy, rim_y[1], 2, True)
    z_y, z_yh = slope(uz, rim_y[2], 2, True)
    x_z, y_z, z_z = slope_z(ux), slope_z(uy), slope_z(uz)
    spread = lam * (x_x + y_y + z_z)
    s_xx = spread + 2.0 * mu * x_x
    s_yy = spread + 2.0 * mu * y_y
    s_zz = spread + 2.0 * mu * z_z
    s_xy = mu * (x_y + y_x)
    s_xz = mu * (x_z + z_x)
    s_yz = mu * (y_z + z_y)
    x_yr = slope(rim_x[0], corner[0], 2, False)
    y_yr = slope(rim_x[1], corner[1], 2, False)
    x_zr, z_zr = slope_z(rim_x[0]), slope_z(rim_x[2])
    s_xx_r = lam_x * (x_xh + y_yr + z_zr) + 2.0 * mu_x * x_xh
    s_xy_r = mu_x * (x_yr + y_xh)
    s_xz_r = mu_x * (x_zr + z_xh)
    x_xc = slope(rim_y[0], corner[0], 1, False)
    y_xc = slope(rim_y[1], corner[1], 1, False)
    y_zc, z_zc = slope_z(rim_y[1]), slope_z(rim_y[2])
    s_yy_c = lam_y * (x_xc + y_yh + z_zc) + 2.0 * mu_y * y_yh
    s_xy_c = mu_y * (x_yh + y_xc)
    s_yz_c = mu_y * (y_zc + z_yh)
    total_x = slope(s_xx, s_xx_r, 1, False) + slope(s_xy, s_xy_c, 2, False) + slope_z(s_xz)
    total_y = slope(s_xy, s_xy_r, 1, False) + slope(s_yy, s_yy_c, 2, False) + slope_z(s_yz)
    total_z = slope(s_xz, s_xz_r, 1, False) + slope(s_yz, s_yz_c, 2, False) + slope_z(s_zz)
    return jnp.stack([total_x, total_y, total_z])


def kernel(
    rows,
    owners,
    u_hbm,
    u_prev_hbm,
    lam_hbm,
    mu_hbm,
    buoy_hbm,
    q_hbm,
    q_prev_hbm,
    arch_hbm,
    stiff_hbm,
    couple_hbm,
    counts_hbm,
    cells_hbm,
    u_last_ref,
    u_before_ref,
    q_last_ref,
    q_before_ref,
    xs0,
    xs1,
    xr0,
    xr1,
    ys,
    yr,
    bs,
    br,
    table,
    u_ref,
    u_prev_ref,
    lam_ref,
    mu_ref,
    buoy_ref,
    q_ref,
    q_prev_ref,
    arch_ref,
    stiff_ref,
    couple_ref,
    counts_ref,
    cells_ref,
    loaded,
    x_send,
    x_recv,
    y_send,
    y_recv,
    b_send,
    b_recv,
):
    r, h = lax.axis_index("gx"), lax.axis_index("gy")
    nz = lam_ref.shape[0]
    slots = q_ref.shape[0]
    capacity = slots // owners
    kinds = stiff_ref.shape[0]
    freedoms = q_ref.shape[1]
    xs, xr = (xs0, xs1), (xr0, xr1)

    def target(direction):
        dx, dy = direction
        there = None
        for d, me, n in ((dx, r, rows), (dy, h, owners)):
            if d:
                ok = me + d < n if d > 0 else me > 0
                there = ok if there is None else there & ok
        return there, (r + dx, h + dy)

    def source(direction):
        return target((-direction[0], -direction[1]))

    peers = X_DIRS + tuple(d for d in Y_DIRS if d[0])

    barrier = pltpu.get_barrier_semaphore()
    arrivals = jnp.int32(owners - 1)
    for step in range(1, owners):
        other = lax.rem(h + step, owners)
        pl.semaphore_signal(barrier, inc=1, device_id=(r, other), device_id_type=MESH)

    for direction in peers:
        there, device = target(direction)
        arrivals = arrivals + there.astype(jnp.int32)

        @pl.when(there)
        def _(device=device):
            pl.semaphore_signal(barrier, inc=1, device_id=device, device_id_type=MESH)

    loads = {}
    for source_ref, ref in (
        (cells_hbm, cells_ref),
        (counts_hbm, counts_ref),
        (arch_hbm, arch_ref),
        (couple_hbm, couple_ref),
        (u_hbm, u_ref),
        (q_hbm, q_ref),
        (lam_hbm, lam_ref),
        (mu_hbm, mu_ref),
        (stiff_hbm, stiff_ref),
        (q_prev_hbm, q_prev_ref),
        (u_prev_hbm, u_prev_ref),
        (buoy_hbm, buoy_ref),
    ):
        copy = pltpu.make_async_copy(source_ref, ref, loaded.at[len(loads)])
        copy.start()
        loads[id(ref)] = copy

    for slot, direction in enumerate(X_DIRS):
        there, _ = source(direction)

        @pl.when(jnp.logical_not(there))
        def _(slot=slot):
            for buffer in xr:
                buffer[slot] = jnp.zeros(buffer.shape[1:], F32)

    for slot, direction in enumerate(Y_DIRS):
        there, _ = source(direction)

        @pl.when(jnp.logical_not(there))
        def _(slot=slot):
            for turn in range(STEPS):
                yr[turn, slot] = jnp.zeros(yr.shape[2:], F32)

    def load(ref):
        loads[id(ref)].wait()
        return ref[...]

    def x_copy(turn, slot, device):
        return pltpu.make_async_remote_copy(
            src_ref=xs[turn].at[slot],
            dst_ref=xr[turn].at[slot],
            send_sem=x_send.at[turn, slot],
            recv_sem=x_recv.at[turn, slot],
            device_id=device,
            device_id_type=MESH,
        )

    def y_copy(turn, slot, device):
        return pltpu.make_async_remote_copy(
            src_ref=ys.at[turn],
            dst_ref=yr.at[turn, slot],
            send_sem=y_send.at[turn, slot],
            recv_sem=y_recv.at[turn, slot],
            device_id=device,
            device_id_type=MESH,
        )

    def b_copy(turn, step):
        other = lax.rem(h + step, owners)
        return pltpu.make_async_remote_copy(
            src_ref=bs.at[turn, other],
            dst_ref=br.at[turn, h],
            send_sem=b_send.at[turn, step],
            recv_sem=b_recv.at[turn, step],
            device_id=(r, other),
            device_id_type=MESH,
        )

    def b_arrival(turn, step):
        other = lax.rem(h + owners - step, owners)
        return pltpu.make_async_remote_copy(
            src_ref=bs.at[turn, other],
            dst_ref=br.at[turn, other],
            send_sem=b_send.at[turn, step],
            recv_sem=b_recv.at[turn, step],
            device_id=(r, other),
            device_id_type=MESH,
        )

    def send_rims(turn):
        for copy, dirs in ((x_copy, X_DIRS), (y_copy, Y_DIRS)):
            for slot, direction in enumerate(dirs):
                there, device = target(direction)

                @pl.when(there)
                def _(copy=copy, slot=slot, device=device):
                    copy(turn, slot, device).start()

    def wait_rims(turn):
        for copy, dirs in ((x_copy, X_DIRS), (y_copy, Y_DIRS)):
            for slot, direction in enumerate(dirs):
                there, device = source(direction)

                @pl.when(there)
                def _(copy=copy, slot=slot, device=device):
                    copy(turn, slot, device).wait_recv()

    def wait_sends(turn):
        for copy, dirs in ((x_copy, X_DIRS), (y_copy, Y_DIRS)):
            for slot, direction in enumerate(dirs):
                there, device = target(direction)

                @pl.when(there)
                def _(copy=copy, slot=slot, device=device):
                    copy(turn, slot, device).wait_send()

        for step in range(1, owners):
            b_copy(turn, step).wait_send()

    def put_rims(turn, fields):
        to_next, to_before = pack_x(fields)
        xs[turn][0] = to_next
        xs[turn][1] = to_before
        tiles = pack_y(fields)
        ys[turn, : tiles.shape[0]] = tiles

    def take_rims(turn, count):
        rim_x = unpack_x(xr[turn][0], xr[turn][1])
        column = (iota((1, 8, 128), 2) & 7) < RIM
        before = jnp.where(column, yr[turn, 4], yr[turn, 5])
        beside = jnp.where(column, yr[turn, 2], yr[turn, 3])
        after = jnp.where(column, yr[turn, 0], yr[turn, 1])
        corner = jnp.where(iota((1, 8, 128), 1) < RIM, after, before)
        return rim_x, unpack_y(beside, count), unpack_y(corner, 3 * nz)


    cells = load(cells_ref)[0].astype(F32)
    wide = (slots, slots * FOOTPRINT_CELLS)
    own = (iota(wide, 1) // FOOTPRINT_CELLS) == iota(wide, 0)
    corner_cell = jnp.min(jnp.where(own, cells, 1e9), axis=1, keepdims=True)
    corner_x = jnp.floor(corner_cell * (1.0 / 128.0))
    corner_y = corner_cell - 128.0 * corner_x
    lane = iota((slots, 128), 1)
    along_y = lane.astype(F32) - corner_y
    window_y = ((along_y == 0.0) | (along_y == 1.0)).astype(F32).astype(BF16)
    along_x = (lane & 7).astype(F32) - corner_x
    part = lane & 31
    slot_row = iota((slots, 1), 0)
    loads[id(counts_ref)].wait()
    row_counts = counts_ref[0, pl.ds(h, 1), :].astype(F32)
    pairs = (slots, owners)
    live_count = jnp.sum(
        jnp.where(iota(pairs, 0) // capacity == iota(pairs, 1), row_counts, 0.0),
        axis=1,
        keepdims=True,
    )
    live = (slot_row % capacity).astype(F32) < live_count
    weight = jnp.where(
        live & ((along_x == 0.0) | (along_x == 1.0)) & (part < 24), 1.0 / FOOTPRINT_CELLS, 0.0
    )
    square = (slots, slots)
    arch = jnp.sum(
        jnp.where(iota(square, 0) == iota(square, 1), load(arch_ref).astype(F32), 0.0),
        axis=1,
        keepdims=True,
    )
    is_kind = [arch == float(a) for a in range(kinds)]
    couple = load(couple_ref)
    coupling = []
    for c in range(3):
        chosen = jnp.zeros((slots, freedoms), F32)
        for a in range(kinds):
            chosen = jnp.where(is_kind[a], couple[c, a : a + 1, :], chosen)
        coupling.append(chosen)

    def surface_motion(field):
        surface = field[:, 0]
        high = surface.astype(BF16).astype(F32)
        nothing = jnp.zeros((8, 128), F32)
        stacked = jnp.concatenate(
            [high.reshape(24, 128), nothing, (surface - high).reshape(24, 128), nothing]
            + [nothing] * 8,
            axis=0,
        ).astype(BF16)
        gathered = lax.dot_general(
            window_y, stacked, (((1,), (1,)), ((), ())), preferred_element_type=F32
        )
        return gathered * weight

    def base_shear(state):
        shear = [jnp.sum(coupling[c] * state, axis=1, keepdims=True) for c in range(3)]
        return jnp.where(part < 8, shear[0], jnp.where(part < 16, shear[1], shear[2]))

    def put_buildings(turn, field, state):
        both = jnp.where(lane < 64, surface_motion(field), base_shear(state))
        both = both.reshape(owners, capacity, 128)
        bs[turn] = both
        br[turn, h] = bs[turn, h]

    def send_buildings(turn):
        for step in range(owners // 2, 0, -1):
            b_copy(turn, step).start()
            if owners - step != step:
                b_copy(turn, owners - step).start()

    def take_buildings(turn):
        for step in range(1, owners):
            b_arrival(turn, step).wait_recv()
        both = br[turn].reshape(slots, 128)
        drive = jnp.zeros((slots, freedoms), F32)
        for c in range(3):
            mine = (lane < 64) & (part >= 8 * c) & (part < 8 * c + 8)
            base = jnp.sum(jnp.where(mine, both, 0.0), axis=1, keepdims=True)
            drive = drive + coupling[c] * base
        pull = both * weight
        high = pull.astype(BF16).astype(F32)
        pull = jnp.where((lane & 32) == 0, high, pull - high)
        spread = lax.dot_general(
            pull.T.astype(BF16), window_y, (((1,), (0,)), ((), ())), preferred_element_type=F32
        )
        force = (spread[64:88] + spread[96:120]).reshape(3, 8, 128)
        return drive, force

    def stiff_term(state):
        high, low = split(state)
        stacked = jnp.concatenate([high.astype(F32), low.astype(F32)], axis=0)
        twice = jnp.concatenate([arch, arch], axis=0)
        spread = jnp.concatenate(
            [jnp.where(twice == float(a), stacked, 0.0).astype(BF16) for a in range(kinds)],
            axis=1,
        )
        product = jnp.dot(spread, table[...], preferred_element_type=F32)
        product = product[:, :freedoms] + product[:, freedoms:]
        return product[:slots] + product[slots:]

    u, q = load(u_ref), load(q_ref)
    put_buildings(0, u, q)
    lam, mu = load(lam_ref) * (1.0 / 144.0), load(mu_ref) * (1.0 / 144.0)
    put_rims(0, jnp.concatenate([u.reshape(3 * nz, 8, 128), lam, mu], axis=0))
    pl.semaphore_wait(barrier, arrivals)
    send_buildings(0)
    send_rims(0)
    stiff_high, stiff_low = split(load(stiff_ref).reshape(kinds * freedoms, freedoms))
    table[:, :freedoms] = stiff_high
    table[:, freedoms:] = stiff_low
    stiff = stiff_term(q)
    u_old, q_old = load(u_prev_ref), load(q_prev_ref)
    gain = load(buoy_ref) * (TIME_STEP * TIME_STEP)
    count = 5 * nz
    lam_mu_x = lam_mu_y = None
    for turn in range(STEPS):
        wait_rims(turn)
        rim_x, rim_y, corner = take_rims(turn, count)
        if turn == 0:
            lam_mu_x, lam_mu_y = rim_x[3 * nz :], rim_y[3 * nz :]
        shape = (3, nz, 8, 128)
        total = divergence(
            u,
            rim_x[: 3 * nz].reshape(shape),
            rim_y[: 3 * nz].reshape(shape),
            corner.reshape(shape),
            lam,
            mu,
            lam_mu_x[:nz],
            lam_mu_x[nz:],
            lam_mu_y[:nz],
            lam_mu_y[nz:],
        )
        drive, force = take_buildings(turn)
        q, q_old = 2.0 * q - q_old + (TIME_STEP * TIME_STEP) * (drive - stiff), q
        total = jnp.concatenate([total[:, :1] + force[:, None], total[:, 1:]], axis=1)
        u, u_old = 2.0 * u - u_old + gain * total, u
        count = 3 * nz
        if turn + 1 < STEPS:
            put_buildings(turn + 1, u, q)
            send_buildings(turn + 1)
            put_rims(turn + 1, u.reshape(3 * nz, 8, 128))
            send_rims(turn + 1)
            u_before_ref[...] = u
            q_before_ref[...] = q
            stiff = stiff_term(q)
    u_last_ref[...] = u
    q_last_ref[...] = q
    for turn in range(STEPS):
        wait_sends(turn)


def shards(
    rows,
    owners,
    u_now,
    u_prev,
    lame_lambda,
    lame_mu,
    buoyancy,
    q_now,
    q_prev,
    archetype,
    stiffness,
    couple,
    counts,
    footprint,
):
    nz = lame_mu.shape[0]
    slots, freedoms = q_now.shape
    capacity = slots // owners
    kinds = stiffness.shape[0]
    pairs = (5 * nz) // 2, (3 * nz) // 2
    vmem = pl.BlockSpec(memory_space=pltpu.VMEM)
    hbm = pl.BlockSpec(memory_space=pltpu.HBM)
    dma = pltpu.SemaphoreType.DMA
    operands = (
        u_now,
        u_prev,
        lame_lambda,
        lame_mu,
        buoyancy,
        q_now,
        q_prev,
        archetype.reshape(1, slots),
        stiffness,
        couple.transpose(1, 0, 2),
        counts,
        footprint,
    )
    results = (
        jax.ShapeDtypeStruct(u_now.shape, F32),
        jax.ShapeDtypeStruct(u_now.shape, F32),
        jax.ShapeDtypeStruct(q_now.shape, F32),
        jax.ShapeDtypeStruct(q_now.shape, F32),
    )
    held = pl.pallas_call(
        functools.partial(kernel, rows, owners),
        out_shape=tuple(pltpu.VMEM(result.shape, result.dtype) for result in results),
        in_specs=[hbm] * len(operands),
        out_specs=(vmem,) * 4,
        scratch_shapes=[
            pltpu.VMEM((2, pairs[0], 8, 128), F32),
            pltpu.VMEM((2, pairs[1], 8, 128), F32),
            pltpu.VMEM((2, pairs[0], 8, 128), F32),
            pltpu.VMEM((2, pairs[1], 8, 128), F32),
            pltpu.VMEM((STEPS, 2, 8, 128), F32),
            pltpu.VMEM((STEPS, len(Y_DIRS), 2, 8, 128), F32),
            pltpu.VMEM((STEPS, owners, capacity, 128), F32),
            pltpu.VMEM((STEPS, owners, capacity, 128), F32),
            pltpu.VMEM((kinds * freedoms, 2 * freedoms), BF16),
        ]
        + [pltpu.VMEM(operand.shape, operand.dtype) for operand in operands]
        + [
            dma((len(operands),)),
            dma((STEPS, 2)),
            dma((STEPS, 2)),
            dma((STEPS, len(Y_DIRS))),
            dma((STEPS, len(Y_DIRS))),
            dma((STEPS, owners)),
            dma((STEPS, owners)),
        ],
        compiler_params=pltpu.CompilerParams(
            collective_id=0, has_side_effects=True, vmem_limit_bytes=60 * 1024 * 1024
        ),
    )(*operands)
    return pl.pallas_call(
        store,
        out_shape=results,
        in_specs=[vmem] * 4,
        out_specs=(hbm,) * 4,
        scratch_shapes=[dma((4,))],
        compiler_params=pltpu.CompilerParams(vmem_limit_bytes=1024 * 1024),
    )(*held)


def store(*refs):
    copies = [
        pltpu.make_async_copy(refs[k], refs[4 + k], refs[8].at[k]) for k in range(4)
    ]
    for copy in copies:
        copy.start()
    for copy in copies:
        copy.wait()


def solution(mesh):
    return jax.shard_map(
        functools.partial(shards, mesh.shape["gx"], mesh.shape["gy"]),
        mesh=mesh,
        in_specs=(
            P(None, None, "gx", "gy"),
            P(None, None, "gx", "gy"),
            P(None, "gx", "gy"),
            P(None, "gx", "gy"),
            P(None, "gx", "gy"),
            P(("gx", "gy"), None),
            P(("gx", "gy"), None),
            P(("gx", "gy")),
            P(),
            P(),
            P("gx", None, None),
            P("gx", "gy", None),
        ),
        out_specs=(
            P(None, None, "gx", "gy"),
            P(None, None, "gx", "gy"),
            P(("gx", "gy"), None),
            P(("gx", "gy"), None),
        ),
        check_vma=False,
    )
```
